256 devices in a mesh: loop: 64 (over z, x_lo, y), tp: 4 (over x_hi, core).
Axes of the slice: x: 4 (x_hi: 2, x_lo: 2; x = x_hi * 2 + x_lo), y: 4, z: 8, core: 2. Of those that a mesh axis runs over, the one named last changes fastest.
Arguments:
- tokens: bfloat16 [32768, 5120], P('loop', 'tp'), may hold values from -6 to 6
- weights: float32 [64, 5120, 1024], P('loop', 'tp'), may hold values from -6 to 6
- gain: float32 [64, 128], P('loop'), may hold values from 0.5 to 1.5
- cotangent: bfloat16 [32768, 1024], P('loop'), may hold values from -6 to 6
- vectors: float32 [64, 4, 1024], P('loop'), may hold values from -6 to 6
Outputs:
- new_weights: float32 [64, 5120, 1024], P('loop', 'tp')
- input_grad: bfloat16 [32768, 5120], P('loop', 'tp')
- new_gain: float32 [64, 128], P('loop')
- new_vectors: float32 [64, 4, 1024], P('loop')
The draws below stay inside these ranges and needn't reach their ends.
All inputs are finite; a program needn't handle non-finite values.
Results may differ from the reference program's by a relative error of at most 0.011.
Values may be sent and summed in bfloat16 or wider, within the bound.
No kernel may reach another device: no remote copies, remote signals or barrier semaphores. Data moves between devices by JAX's collectives and lax.ppermute only.
A program may use at most 128 MiB of HBM per device.

```python
import jax
import jax.numpy as jnp
from jax import lax

D = 5120
HEAD = 128
ROWS = 512
RANK = 4
KVW = 1024
REPLICAS = 64
ALLROWS = 32768


def levels(key, extent, pieces, least, high):
    loudness = 1.0
    for axis_at, parts in pieces:
        heights = jax.random.uniform(jax.random.fold_in(jax.random.fold_in(key, 6), axis_at), (parts,), jnp.float32, least / len(pieces), high / len(pieces))
        loudness = loudness * jnp.repeat(jnp.exp(heights), extent[axis_at] // parts).reshape((-1,) + (1,) * (len(extent) - 1 - axis_at))
    return loudness


def gaussian(stream_key, dims, deviation, bound, cuts=(), kind=jnp.bfloat16):
    drawn = jax.random.normal(stream_key, dims, jnp.float32) * deviation
    if len(cuts) > 0:
        drawn = levels(stream_key, dims, cuts, -0.22, 0.18) * drawn
    return jnp.clip(drawn, min=-bound, max=bound).astype(kind)


def setup_inputs(seed: int = 0) -> dict:
    splits = jax.random.split(jax.random.key(seed), 6)
    return {
        "tokens": gaussian(splits[0], (ALLROWS, D), 1.0, 6.0, ((0, 64), (1, 4))),
        "weights": gaussian(splits[1], (REPLICAS, D, KVW), 1.0, 6.0, ((0, 64), (1, 4)), jnp.float32),
        "gain": jnp.clip(1.0 + 0.1 * jax.random.normal(splits[2], (REPLICAS, HEAD), jnp.float32), 0.5, 1.5),
        "cotangent": gaussian(splits[3], (ALLROWS, KVW), 1.0, 6.0, ((0, 64),)),
        "vectors": gaussian(splits[4], (REPLICAS, RANK, KVW), 1.0, 6.0, ((0, 64),), jnp.float32),
    }


HIGH = lax.Precision.HIGHEST

def lower_solve(lower, rhs):
    return lax.linalg.triangular_solve(lower, rhs, left_side=True, lower=True)

def norm_back(keys, gain, upstream):
    rows = keys.shape[0]
    split = keys.reshape(rows, -1, gain.shape[0])
    inv = lax.rsqrt(lax.optimization_barrier(jnp.mean(split * split, axis=-1, keepdims=True)) + 1e-06)
    unit = split * inv
    grad_up = upstream.astype(jnp.float32).reshape(split.shape)
    gain_grad = lax.optimization_barrier(jnp.sum(grad_up * unit, axis=(0, 1)))
    scaled = grad_up * gain
    key_grad = inv * (scaled - unit * lax.optimization_barrier(jnp.mean(scaled * unit, axis=-1, keepdims=True)))
    return (key_grad.reshape(rows, -1), gain_grad)

def replica_step(args):
    tokens_r, weight_r, gain_r, upstream = args
    scale = D ** (-0.5)
    wb = weight_r.astype(jnp.bfloat16)
    keys = jnp.dot(tokens_r.astype(jnp.float32), wb.astype(jnp.float32), preferred_element_type=jnp.float32) * scale
    key_grad, gain_grad = norm_back(keys, gain_r, upstream)
    kgb = key_grad.astype(jnp.bfloat16)
    input_grad = (jnp.dot(kgb.astype(jnp.float32), wb.T.astype(jnp.float32), preferred_element_type=jnp.float32) * scale).astype(jnp.bfloat16)
    weight_grad = jnp.dot(tokens_r.T.astype(jnp.float32), kgb.astype(jnp.float32), preferred_element_type=jnp.float32) * scale
    return (weight_r - 0.1 * weight_grad, input_grad, gain_r - 0.002 * gain_grad)

def reference(tokens, weights, gain, cotangent, vectors):
    count = weights.shape[0]
    tok = tokens.reshape(count, ROWS, D)
    cot = cotangent.reshape(count, ROWS, KVW)
    stepped, input_grad, new_gain = lax.map(replica_step, (tok, weights, gain, cot))

    def edge(index):
        here = stepped[index]
        there = stepped[(index + 1) % count]
        qvec = vectors[index]
        rows = jnp.dot(qvec, here.T, precision=HIGH) - jnp.dot(qvec, there.T, precision=HIGH)
        lower = jnp.linalg.cholesky(jnp.dot(rows, rows.T, precision=HIGH))
        unit_rows = lower_solve(lower, rows)
        back = jnp.dot(unit_rows, here, precision=HIGH) - jnp.dot(unit_rows, there, precision=HIGH)
        return (unit_rows, back)
    unit_all, new_vectors = lax.map(edge, jnp.arange(count, dtype=jnp.int32))

    def mix(index):
        left = (index + count - 1) % count
        right_term = jnp.dot(unit_all[index].T, new_vectors[index], precision=HIGH)
        left_term = jnp.dot(unit_all[left].T, new_vectors[left], precision=HIGH)
        return stepped[index] - 1.0 / 3.0 * (right_term - left_term)
    new_weights = lax.map(mix, jnp.arange(count, dtype=jnp.int32))
    return (new_weights, input_grad.reshape(count * ROWS, D), new_gain, new_vectors)
```

```python
import functools

import jax
import jax.numpy as jnp
from jax import lax
from jax.experimental import pallas as pl
from jax.experimental.pallas import tpu as pltpu
from jax.sharding import PartitionSpec as P

F32 = jnp.float32
BF16 = jnp.bfloat16
MIB = 1024 * 1024
VM = pl.BlockSpec(memory_space=pltpu.VMEM)
ANY = pl.BlockSpec(memory_space=pl.ANY)
NT = (((1,), (1,)), ((), ()))


def in_vmem(x):
    return pltpu.with_memory_space_constraint(x, pltpu.VMEM)


def call(body, args, outs, scratch=(), limit=24, flops=0, nbytes=0, spaces=None, out_spaces=None):
    spaces = spaces or (True,) * len(args)
    out_spaces = out_spaces or (True,) * len(outs)
    return pl.pallas_call(
        body,
        out_shape=[
            pltpu.VMEM(shape, dtype) if inside else jax.ShapeDtypeStruct(shape, dtype)
            for (shape, dtype), inside in zip(outs, out_spaces)
        ],
        in_specs=[VM if inside else ANY for inside in spaces],
        out_specs=[VM if inside else ANY for inside in out_spaces],
        scratch_shapes=list(scratch),
        compiler_params=pltpu.CompilerParams(vmem_limit_bytes=limit * MIB),
        cost_estimate=pl.CostEstimate(flops=flops, bytes_accessed=nbytes, transcendentals=0),
    )(*[in_vmem(a) if inside else a for a, inside in zip(args, spaces)])


def dot(a, b, dims=(((1,), (0,)), ((), ()))):
    return lax.dot_general(a, b, dims, preferred_element_type=F32)


def split(x):
    hi = x.astype(BF16)
    return hi, (x - hi.astype(F32)).astype(BF16)


def core_index():
    return lax.rem(lax.axis_index("tp"), 2)


def half_at(which, half):
    return pl.ds(pl.multiple_of(which * half, 128), half)


def sent_kernel(tok, w, tok_v, w_s, hi_s, part, tok_sem, w_sem):
    half = w_s.shape[1]
    depth = w_s.shape[0]
    steps = w_sem.shape[0]
    k = depth // steps
    cols = half_at(1 - core_index(), half)
    tok_copies, w_copies = [], []
    for j in range(steps):
        at = pl.ds(j * k, k)
        tok_copies.append(pltpu.make_async_copy(tok.at[:, at], tok_v.at[:, at], tok_sem.at[j]))
        w_copies.append(pltpu.make_async_copy(w.at[at, cols], w_s.at[at], w_sem.at[j]))
        tok_copies[j].start()
        w_copies[j].start()
    acc = None
    for j in range(steps):
        tok_copies[j].wait()
        w_copies[j].wait()
        hi = w_s[j * k : (j + 1) * k].astype(BF16)
        hi_s[j * k : (j + 1) * k] = hi
        term = dot(tok_v[:, j * k : (j + 1) * k], hi)
        acc = term if acc is None else acc + term
    part[...] = acc.astype(BF16)


def kept_kernel(tok_v, w, w_k, hi_k, part, w_sem):
    half = w_k.shape[1]
    depth = w_k.shape[0]
    steps = w_sem.shape[0]
    k = depth // steps
    cols = half_at(core_index(), half)
    w_copies = []
    for j in range(steps):
        at = pl.ds(j * k, k)
        w_copies.append(pltpu.make_async_copy(w.at[at, cols], w_k.at[at], w_sem.at[j]))
        w_copies[j].start()
    acc = None
    for j in range(steps):
        w_copies[j].wait()
        hi = w_k[j * k : (j + 1) * k].astype(BF16)
        hi_k[j * k : (j + 1) * k] = hi
        term = dot(tok_v[:, j * k : (j + 1) * k], hi)
        acc = term if acc is None else acc + term
    part[...] = acc


def chip_sum_kernel(part, got, out):
    out[...] = (part[...] + got[...].astype(F32)).astype(BF16)


def shadow_kernel(tok_v, w_s, w_k, vec, left_vec, proj, tok_t):
    half = w_s.shape[1]
    c = core_index()
    total = None
    for w_half, which in ((w_s, 1 - c), (w_k, c)):
        at = half_at(which, half)
        q = jnp.concatenate([vec[:, at], left_vec[:, at]], axis=0)
        q_hi, q_lo = split(q)
        w_hi, w_lo = split(w_half[...])
        term = dot(q_hi, w_hi, NT) + dot(q_lo, w_hi, NT) + dot(q_hi, w_lo, NT)
        total = term if total is None else total + term
    proj[...] = total
    tok_t[...] = tok_v[...].T


def norm_kernel(scale, own, got, cot, gain, kg, gain_grad):
    head = gain.shape[1]
    heads = own.shape[1] // head
    half = own.shape[1]
    at = half_at(core_index(), half)
    keys_all = (own[...].astype(F32) + got[...].astype(F32)) * scale
    up_all = cot[:, at].astype(F32)
    g = gain[...]
    total = None
    for h in range(heads):
        cols = slice(h * head, (h + 1) * head)
        keys = keys_all[:, cols]
        up = up_all[:, cols]
        gh = up * g
        inv = lax.rsqrt(jnp.mean(keys * keys, axis=-1, keepdims=True) + 1e-6)
        along = jnp.mean(gh * keys, axis=-1, keepdims=True)
        unit = keys * inv
        kg[:, cols] = (inv * (gh - unit * (inv * along))).astype(BF16)
        part = jnp.sum(up * unit, axis=0, keepdims=True)
        total = part if total is None else total + part
    gain_grad[...] = total


def project_kernel(rate, kg_k, kg_s, vec, left_vec, proj0, tok_v, right, left):
    half = kg_k.shape[1]
    c = core_index()
    g = None
    for kg, which in ((kg_k, c), (kg_s, 1 - c)):
        at = half_at(which, half)
        q_hi, q_lo = split(jnp.concatenate([vec[:, at], left_vec[:, at]], axis=0))
        term = dot(q_hi, kg[...], NT) + dot(q_lo, kg[...], NT)
        g = term if g is None else g + term
    g_hi, g_lo = split(g)
    proj = proj0[...] - rate * (dot(g_hi, tok_v[...]) + dot(g_lo, tok_v[...]))
    rank = right.shape[0]
    right[...] = proj[:rank]
    left[...] = proj[rank:]


def step_kernel(rate, tok_t, kg, w, out):
    out[...] = w[...] - rate * dot(tok_t[...], kg[...])


def input_kernel(scale, kg_k, kg_s, hi_k, hi_s, out):
    out[...] = ((dot(kg_k[...], hi_k[...], NT) + dot(kg_s[...], hi_s[...], NT)) * scale).astype(BF16)


def back_kernel(right, left, got_right, got_left, s_k, s_s, gain_grad, rows_out, payload):
    half = s_k.shape[1]
    c = core_index()
    rows = jnp.concatenate([right[...] - got_right[...], got_left[...] - left[...]], axis=0)
    rows_out[...] = rows
    r_hi, r_lo = split(rows)
    for s, which in ((s_k, c), (s_s, 1 - c)):
        s_hi, s_lo = split(s[...])
        payload[:, half_at(which, half)] = dot(r_hi, s_hi) + dot(r_lo, s_hi) + dot(r_hi, s_lo)
    n = rows.shape[0]
    gram = lax.dot_general(rows, rows, NT, precision=lax.Precision.HIGHEST, preferred_element_type=F32)
    payload[:, 2 * half : 2 * half + 128] = jnp.concatenate([gram, jnp.zeros((n, 128 - n), F32)], axis=1)
    payload[:, 2 * half + 128 :] = jnp.broadcast_to(gain_grad[...], (n, 128))


def pair_kernel(mine, other, gain, total, aside, new_gain):
    rank = aside.shape[0]
    width = aside.shape[1]
    both = mine[...] + other[...]
    total[...] = both[:, : width + 128]
    c = core_index()
    aside[...] = jnp.where(c == 0, both[:rank, :width], both[rank:, :width])
    new_gain[...] = gain[...] - 0.002 * both[0:1, width + 128 :]


def edge_kernel(total, other, got, got_far, mine, gram):
    rank, width = mine.shape
    whole = total[...] + other[...]
    c = core_index()
    near = jnp.where(c == 0, whole[rank:, :width], whole[:rank, :width])
    far = got[...] + got_far[...]
    mine[...] = jnp.where(c == 0, far - near, near - far)
    gram[...] = whole[:, width:]


def whiten_kernel(rank, gram, rows, inverse, unit):
    n = gram.shape[0]
    width = gram.shape[1]
    lane = lax.broadcasted_iota(jnp.int32, (rank, width), 1)
    row = lax.broadcasted_iota(jnp.int32, (rank, width), 0)
    parts = []
    for e in range(n // rank):
        a = gram[e * rank : (e + 1) * rank]
        a = jnp.where((lane >= e * rank) & (lane < (e + 1) * rank), a, 0.0)
        a = jnp.where(lane == n + e * rank + row, 1.0, a)
        for i in range(rank):
            col = a[:, e * rank + i : e * rank + i + 1]
            pivot = lax.rsqrt(col[i : i + 1])
            line = a[i : i + 1] * pivot
            a = jnp.where(row == i, line, jnp.where(row > i, a - (col * pivot) * line, a))
        parts.append(a)
    both = jnp.concatenate(parts, axis=0)
    inverse[...] = both
    unit[...] = apply_inverse(both, rows[...], n)


def apply_inverse(both, x, n):
    total = None
    for j in range(n):
        term = both[:, n + j : n + j + 1] * x[j : j + 1]
        total = term if total is None else total + term
    return total


def mix_kernel(s_k, s_s, unit, inverse, mine, other, out, new_vec, stage, sem):
    rank, width = mine.shape
    half = s_k.shape[1]
    depth = s_k.shape[0]
    steps = sem.shape[0]
    k = depth // steps
    n = 2 * rank
    c = core_index()
    a, b = mine[...], other[...]
    back = jnp.concatenate([jnp.where(c == 0, b, a), jnp.where(c == 0, a, b)], axis=0)
    nv = apply_inverse(inverse[...], back, n)
    new_vec[...] = nv[:rank]
    sign = jnp.where(lax.broadcasted_iota(jnp.int32, (n, width), 0) < rank, 1.0 / 3.0, -1.0 / 3.0)
    v_hi, v_lo = split(nv * sign)
    stacked = jnp.concatenate([v_hi, v_lo, v_hi], axis=0)
    u_hi, u_lo = split(unit[...])
    lhs = jnp.concatenate([u_hi, u_hi, u_lo], axis=0)
    stage_v = stage
    copies = []
    for j in range(steps):
        at = slice(j * k, (j + 1) * k)
        delta = lax.dot_general(lhs[:, at], stacked, (((0,), (0,)), ((), ())), preferred_element_type=F32)
        low = jnp.where(c == 0, s_k[at], s_s[at])
        high = jnp.where(c == 0, s_s[at], s_k[at])
        stage_v[at, :half] = low - delta[:, :half]
        stage_v[at, half:] = high - delta[:, half:]
        copies.append(pltpu.make_async_copy(stage_v.at[pl.ds(j * k, k)], out.at[pl.ds(j * k, k)], sem.at[j]))
        copies[j].start()
    for j in range(steps):
        copies[j].wait()


def shards(tokens, weights, gain, cotangent, vectors):
    rows, depth = tokens.shape
    width = weights.shape[2]
    half = width // 2
    rank = vectors.shape[1]
    tp = lax.axis_size("tp")
    loop = lax.axis_size("loop")
    scale = (depth * tp) ** -0.5
    rate = 0.1 * scale
    weight = weights[0]
    vec = vectors[0]
    core = [(i, i ^ 1) for i in range(tp)]
    chip = [(i, i ^ 2) for i in range(tp)]
    right = [(i, (i + 1) % loop) for i in range(loop)]
    left = [(i, (i - 1) % loop) for i in range(loop)]
    along, along_far = [], []
    for i in range(loop):
        for t in range(tp):
            to = (i + 1) % loop if t % 2 == 0 else (i - 1) % loop
            along.append((i * tp + t, to * tp + t))
            along_far.append((i * tp + t, to * tp + (t ^ 2)))
    everyone = ("loop", "tp")

    left_vec = lax.ppermute(vec, "loop", right)
    steps = 5
    dma = pltpu.SemaphoreType.DMA
    half_flops = 2 * rows * depth * half
    tok_v, w_s, hi_s, part_s = call(
        sent_kernel,
        (tokens, weight),
        [((rows, depth), BF16), ((depth, half), F32), ((depth, half), BF16), ((rows, half), BF16)],
        [dma((steps,)), dma((steps,))],
        spaces=(False, False),
        flops=half_flops,
        nbytes=4 * MIB,
    )
    from_core = lax.ppermute(part_s, "tp", core)
    w_k, hi_k, part_k = call(
        kept_kernel,
        (tok_v, weight),
        [((depth, half), F32), ((depth, half), BF16), ((rows, half), F32)],
        [dma((steps,))],
        spaces=(True, False),
        flops=half_flops,
        nbytes=3 * MIB,
    )
    (chip_part,) = call(chip_sum_kernel, (part_k, from_core), [((rows, half), BF16)], nbytes=2 * MIB)
    from_chip = lax.ppermute(chip_part, "tp", chip)
    proj0, tok_t = call(
        shadow_kernel,
        (tok_v, w_s, w_k, vec, left_vec),
        [((2 * rank, depth), F32), ((depth, rows), BF16)],
        flops=half_flops,
        nbytes=8 * MIB,
    )
    kg_k, gain_grad = call(
        functools.partial(norm_kernel, scale),
        (chip_part, from_chip, cotangent, gain),
        [((rows, half), BF16), (gain.shape, F32)],
        nbytes=2 * MIB,
    )
    kg_s = lax.ppermute(kg_k, "tp", core)
    (s_k,) = call(
        functools.partial(step_kernel, rate),
        (tok_t, kg_k, w_k),
        [((depth, half), F32)],
        flops=half_flops,
        nbytes=6 * MIB,
    )
    proj_right, proj_left = call(
        functools.partial(project_kernel, rate),
        (kg_k, kg_s, vec, left_vec, proj0, tok_v),
        [((rank, depth), F32), ((rank, depth), F32)],
        nbytes=2 * MIB,
    )
    got_left = lax.ppermute(proj_right, "loop", right)
    got_right = lax.ppermute(proj_left, "loop", left)
    (s_s,) = call(
        functools.partial(step_kernel, rate),
        (tok_t, kg_s, w_s),
        [((depth, half), F32)],
        flops=half_flops,
        nbytes=6 * MIB,
    )
    (input_grad,) = call(
        functools.partial(input_kernel, scale),
        (kg_k, kg_s, hi_k, hi_s),
        [((rows, depth), BF16)],
        flops=2 * half_flops,
        nbytes=5 * MIB,
    )
    edge_rows, payload = call(
        back_kernel,
        (proj_right, proj_left, got_right, got_left, s_k, s_s, gain_grad),
        [((2 * rank, depth), F32), ((2 * rank, width + 256), F32)],
        nbytes=6 * MIB,
    )
    other_core = lax.ppermute(payload, "tp", core)
    pair, aside, new_gain = call(
        pair_kernel,
        (payload, other_core, gain),
        [((2 * rank, width + 128), F32), ((rank, width), F32), (gain.shape, F32)],
    )
    got_near = lax.ppermute(aside, everyone, along)
    got_far = lax.ppermute(aside, everyone, along_far)
    other_chip = lax.ppermute(pair, "tp", chip)
    mine, gram = call(
        edge_kernel,
        (pair, other_chip, got_near, got_far),
        [((rank, width), F32), ((2 * rank, 128), F32)],
    )
    other = lax.ppermute(mine, "tp", core)
    inverse, unit = call(
        functools.partial(whiten_kernel, rank),
        (gram, edge_rows),
        [((2 * rank, 128), F32), ((2 * rank, depth), F32)],
    )
    new_weights, new_vec = call(
        mix_kernel,
        (s_k, s_s, unit, inverse, mine, other),
        [((depth, width), F32), ((rank, width), F32)],
        [pltpu.VMEM((depth, width), F32), dma((steps,))],
        out_spaces=(False, True),
        nbytes=10 * MIB,
    )
    return (new_weights[None], input_grad, new_gain, new_vec[None])


def solution(mesh):
    return jax.shard_map(
        shards,
        mesh=mesh,
        in_specs=(
            P("loop", "tp"),
            P("loop", "tp", None),
            P("loop", None),
            P("loop", None),
            P("loop", None, None),
        ),
        out_specs=(P("loop", "tp", None), P("loop", "tp"), P("loop", None), P("loop", None, None)),
        check_vma=False,
    )
```

```python
import functools

import jax
import jax.numpy as jnp
from jax import lax
from jax.experimental import pallas as pl
from jax.experimental.pallas import tpu as pltpu
from jax.sharding import PartitionSpec as P

F32 = jnp.float32
BF16 = jnp.bfloat16
MIB = 1024 * 1024
VM = pl.BlockSpec(memory_space=pltpu.VMEM)
ANY = pl.BlockSpec(memory_space=pl.ANY)
NT = (((1,), (1,)), ((), ()))


def in_vmem(x):
    return pltpu.with_memory_space_constraint(x, pltpu.VMEM)


def in_hbm(x):
    return pltpu.with_memory_space_constraint(x, pltpu.HBM)


def call(body, args, outs, scratch=(), limit=24, nbytes=1, spaces=None, out_spaces=None, aliases=None):
    spaces = spaces or (True,) * len(args)
    out_spaces = out_spaces or (True,) * len(outs)
    return pl.pallas_call(
        body,
        out_shape=[
            pltpu.VMEM(shape, dtype) if inside else pltpu.HBM(shape, dtype)
            for (shape, dtype), inside in zip(outs, out_spaces)
        ],
        in_specs=[VM if inside else ANY for inside in spaces],
        out_specs=[VM if inside else ANY for inside in out_spaces],
        scratch_shapes=list(scratch),
        input_output_aliases=aliases or {},
        compiler_params=pltpu.CompilerParams(vmem_limit_bytes=limit * MIB),
        cost_estimate=pl.CostEstimate(flops=400 * nbytes, bytes_accessed=nbytes, transcendentals=0),
    )(*[in_vmem(a) if inside else in_hbm(a) for a, inside in zip(args, spaces)])


def dot(a, b, dims=(((1,), (0,)), ((), ()))):
    return lax.dot_general(a, b, dims, preferred_element_type=F32)


def split(x):
    hi = x.astype(BF16)
    return hi, (x - hi.astype(F32)).astype(BF16)


def core_index():
    return lax.rem(lax.axis_index("tp"), 2)


def chunk_at(kept, i, wide):
    c = core_index()
    which = c if kept else 1 - c
    return pl.ds(pl.multiple_of(which * (2 * wide) + i * wide, 128), wide)


def half_in(w, to, kept, sems):
    half = to.shape[1]
    steps = sems.shape[0]
    k = to.shape[0] // steps
    c = core_index()
    cols = pl.ds(pl.multiple_of((c if kept else 1 - c) * half, 128), half)
    copies = []
    for j in range(steps):
        at = pl.ds(j * k, k)
        copies.append(pltpu.make_async_copy(w.at[at, cols], to.at[at], sems.at[j]))
        copies[j].start()
    return copies


def partial(tok_v, w_v, hi_v, copies):
    steps = len(copies)
    k = w_v.shape[0] // steps
    acc = None
    for j in range(steps):
        copies[j].wait()
        at = slice(j * k, (j + 1) * k)
        hi = w_v[at].astype(BF16)
        hi_v[at] = hi
        term = dot(tok_v[:, at], hi)
        acc = term if acc is None else acc + term
    return acc


def first_kernel(tok, w, tok_v, w_s, hi_s, part, tok_sem, w_sem):
    tok_copy = pltpu.make_async_copy(tok, tok_v, tok_sem)
    tok_copy.start()
    copies = half_in(w, w_s, False, w_sem)
    tok_copy.wait()
    part[...] = partial(tok_v, w_s, hi_s, copies).astype(BF16)


def own_kernel(tok_v, w, w_k, hi_k, own, w_sem):
    own[...] = partial(tok_v, w_k, hi_k, half_in(w, w_k, True, w_sem))


def chip_sum_kernel(own, got, out0, out1):
    wide = out0.shape[1]
    out0[...] = (own[:, :wide] + got[:, :wide].astype(F32)).astype(BF16)
    out1[...] = (own[:, wide:] + got[:, wide:].astype(F32)).astype(BF16)


def halves_of(vec, left_vec, at):
    hi, lo = split(jnp.concatenate([vec[:, at], left_vec[:, at]], axis=0))
    return jnp.concatenate([hi, lo], axis=0)


def shadow_kernel(tok_v, w_k, w_s, vec, left_vec, _, proj, tok_t):
    wide = w_k.shape[1] // 2
    n = proj.shape[0]
    total = None
    for w, kept, i in ((w_k, True, 0), (w_k, True, 1), (w_s, False, 0), (w_s, False, 1)):
        q = halves_of(vec, left_vec, chunk_at(kept, i, wide))
        w_hi, w_lo = split(w[:, i * wide : (i + 1) * wide])
        both = dot(q, w_hi, NT)
        term = both[:n] + both[n:] + dot(q[:n], w_lo, NT)
        total = term if total is None else total + term
    proj[...] = total
    tok_t[...] = tok_v[...].T


def norm_kernel(scale, i, own, got, cot, gain, vec, left_vec, on_keys_in, gain_in, _, kg, on_keys, gain_grad, passed):
    head = gain.shape[1]
    wide = own.shape[1]
    n = on_keys.shape[0]
    g = gain[...]
    start = chunk_at(True, i, wide).start
    total = gain_in[...]
    for h in range(wide // head):
        cols = slice(h * head, (h + 1) * head)
        keys = (own[:, cols].astype(F32) + got[:, cols].astype(F32)) * scale
        up = cot[:, pl.ds(pl.multiple_of(start + h * head, head), head)].astype(F32)
        gh = up * g
        inv = lax.rsqrt(jnp.mean(keys * keys, axis=-1, keepdims=True) + 1e-6)
        along = jnp.mean(gh * keys, axis=-1, keepdims=True)
        unit = keys * inv
        kg[:, cols] = (inv * (gh - unit * (inv * along))).astype(BF16)
        total = total + jnp.sum(up * unit, axis=0, keepdims=True)
    gain_grad[...] = total
    both = dot(halves_of(vec, left_vec, chunk_at(True, i, wide)), kg[...], NT)
    on_keys[...] = on_keys_in[...] + both[:n] + both[n:]


def odd_replica():
    return lax.rem(lax.axis_index("loop"), 2) == 1


def project_kernel(rate, mine, other, proj0, tok_v, kg_0, kg_1, first, second, out, *passed):
    hi, lo = split(mine[...] + other[...])
    rank = first.shape[0]
    n = 2 * rank
    both = dot(jnp.concatenate([hi, lo], axis=0), tok_v[...])
    proj = proj0[...] - rate * (both[:n] + both[n:])
    out[...] = proj
    odd = odd_replica()
    first[...] = jnp.where(odd, proj[:rank], proj[rank:])
    second[...] = jnp.where(odd, proj[rank:], proj[:rank])


def step_kernel(rate, i, tok_t, kg, w, out, out_hi, out_lo, kg_out):
    wide = kg.shape[1]
    stepped = w[:, i * wide : (i + 1) * wide] - rate * dot(tok_t[...], kg[...])
    out[...] = stepped
    hi, lo = split(stepped)
    out_hi[...] = hi
    out_lo[...] = lo


def input_kernel(scale, kg_k0, kg_k1, kg_s0, kg_s1, hi_k, hi_s, _, out, stage, sem):
    wide = kg_k0.shape[1]
    steps = sem.shape[0]
    k = stage.shape[1] // steps
    copies = []
    for j in range(steps):
        at = slice(j * k, (j + 1) * k)
        total = None
        for kg, hi, i in ((kg_k0, hi_k, 0), (kg_k1, hi_k, 1), (kg_s0, hi_s, 0), (kg_s1, hi_s, 1)):
            term = dot(kg[...], hi[at, i * wide : (i + 1) * wide], NT)
            total = term if total is None else total + term
        stage[:, at] = (total * scale).astype(BF16)
        copies.append(pltpu.make_async_copy(stage.at[:, pl.ds(j * k, k)], out.at[:, pl.ds(j * k, k)], sem.at[j]))
        copies[j].start()
    for j in range(steps):
        copies[j].wait()


def rows_kernel(proj, got_first, got_second, _0, _1, rows_out, gram_out):
    n = proj.shape[0]
    rank = n // 2
    odd = odd_replica()
    got_right = jnp.where(odd, got_first[...], got_second[...])
    got_left = jnp.where(odd, got_second[...], got_first[...])
    rows = jnp.concatenate([proj[:rank] - got_right, got_left - proj[rank:]], axis=0)
    rows_out[...] = rows
    gram = lax.dot_general(rows, rows, NT, precision=lax.Precision.HIGHEST, preferred_element_type=F32)
    gram_out[...] = jnp.concatenate([gram, jnp.zeros((n, 128 - n), F32)], axis=1)


def back_kernel(rows, gram, gain_grad, *refs):
    *blocks, out = refs
    wide = blocks[0].shape[1]
    width = 4 * wide
    n = rows.shape[0]
    r_hi, r_lo = split(rows[...])
    r = jnp.concatenate([r_hi, r_lo], axis=0)
    for j, (kept, i) in enumerate(((True, 0), (True, 1), (False, 0), (False, 1))):
        s_hi, s_lo = blocks[2 * j], blocks[2 * j + 1]
        both = dot(r, s_hi[...])
        out[:, chunk_at(kept, i, wide)] = both[:n] + both[n:] + dot(r_hi, s_lo[...])
    out[:, width : width + 128] = gram[...]
    out[:, width + 128 :] = jnp.broadcast_to(gain_grad[...], (n, 128))


def pair_kernel(mine, other, pair, gain_grad):
    both = mine[...] + other[...]
    width = pair.shape[1]
    pair[...] = both[:, :width]
    gain_grad[...] = both[0:1, width:]


def sum_kernel(mine, other, aside, keep, gram):
    rank, width = aside.shape
    whole = mine[...] + other[...]
    first = core_index() == 0
    aside[...] = jnp.where(first, whole[:rank, :width], whole[rank:, :width])
    keep[...] = jnp.where(first, whole[rank:, :width], whole[:rank, :width])
    gram[...] = whole[:, width:]


def edge_kernel(keep, got, _0, _1, out):
    out[...] = jnp.where(core_index() == 0, got[...] - keep[...], keep[...] - got[...])


def inverse_factor(gram, rank):
    n = gram.shape[0]
    width = gram.shape[1]
    lane = lax.broadcasted_iota(jnp.int32, (rank, width), 1)
    row = lax.broadcasted_iota(jnp.int32, (rank, width), 0)
    parts = []
    for e in range(n // rank):
        a = gram[e * rank : (e + 1) * rank]
        a = jnp.where((lane >= e * rank) & (lane < (e + 1) * rank), a, 0.0)
        a = jnp.where(lane == n + e * rank + row, 1.0, a)
        for i in range(rank):
            col = a[:, e * rank + i : e * rank + i + 1]
            pivot = lax.rsqrt(col[i : i + 1])
            line = a[i : i + 1] * pivot
            a = jnp.where(row == i, line, jnp.where(row > i, a - (col * pivot) * line, a))
        parts.append(a)
    return jnp.concatenate(parts, axis=0)


def apply_inverse(both, x, n):
    total = None
    for j in range(n):
        term = both[:, n + j : n + j + 1] * x[j : j + 1]
        total = term if total is None else total + term
    return total


def whiten_kernel(rank, gram, rows, gain, gain_grad, inverse, lhs, new_gain, stage, sem):
    stage[...] = gain[...] - 0.002 * gain_grad[...]
    copy = pltpu.make_async_copy(stage, new_gain, sem)
    copy.start()
    both = inverse_factor(gram[...], rank)
    inverse[...] = both
    u_hi, u_lo = split(apply_inverse(both, rows[...], 2 * rank))
    lhs[...] = jnp.concatenate([u_hi, u_hi, u_lo, jnp.zeros_like(u_hi)], axis=0).T
    copy.wait()


def mix_kernel(s_k0, s_k1, s_s0, s_s1, inverse, lhs, mine, other, out, new_vec, stage, vec_stage, right_side, sem, vec_sem):
    rank, width = vec_stage.shape
    depth, wide = s_k0.shape
    n = 2 * rank
    first = core_index() == 0
    a, b = mine[...], other[...]
    back = jnp.concatenate([jnp.where(first, b, a), jnp.where(first, a, b)], axis=0)
    nv = apply_inverse(inverse[...], back, n)
    sign = jnp.where(lax.broadcasted_iota(jnp.int32, (n, width), 0) < rank, 1.0 / 3.0, -1.0 / 3.0)
    v_hi, v_lo = split(nv * sign)
    right_side[...] = jnp.concatenate([v_hi, v_lo, v_hi, jnp.zeros_like(v_hi)], axis=0)
    vec_stage[...] = nv[:rank]
    vec_copy = pltpu.make_async_copy(vec_stage, new_vec, vec_sem)
    vec_copy.start()
    parts = sem.shape[0]
    k = depth // parts
    copies = []
    for p in range(parts):
        at = slice(p * k, (p + 1) * k)
        for s, kept, i in ((s_k0, True, 0), (s_k1, True, 1), (s_s0, False, 0), (s_s1, False, 1)):
            cols = chunk_at(kept, i, wide)
            stage[at, cols] = s[at] - dot(lhs[at], right_side[:, cols])
        copies.append(pltpu.make_async_copy(stage.at[pl.ds(p * k, k)], out.at[pl.ds(p * k, k)], sem.at[p]))
        copies[p].start()
    for copy in copies:
        copy.wait()
    vec_copy.wait()


def shards(tokens, weights, gain, cotangent, vectors):
    rows, depth = tokens.shape
    width = weights.shape[2]
    half = width // 2
    wide = half // 2
    rank = vectors.shape[1]
    n = 2 * rank
    tp = lax.axis_size("tp")
    loop = lax.axis_size("loop")
    scale = (depth * tp) ** -0.5
    rate = 0.1 * scale
    weight = weights[0]
    vec = vectors[0]
    core = [(i, i ^ 1) for i in range(tp)]
    chip = [(i, i ^ 2) for i in range(tp)]
    right = [(i, (i + 1) % loop) for i in range(loop)]
    odd_edges = [(i, (i + 1 if i % 2 else i - 1) % loop) for i in range(loop)]
    even_edges = [(i, i ^ 1) for i in range(loop)]
    along = [
        (i * tp + t, ((i + 1) % loop if t % 2 == 0 else (i - 1) % loop) * tp + t) for i in range(loop) for t in range(tp)
    ]
    dma = pltpu.SemaphoreType.DMA
    block, block16, keys16 = ((depth, wide), F32), ((depth, wide), BF16), ((rows, wide), BF16)
    steps = 5

    tok_v, w_s, hi_s, part = call(
        first_kernel,
        (tokens, weight),
        [((rows, depth), BF16), ((depth, half), F32), ((depth, half), BF16), ((rows, half), BF16)],
        [dma, dma((steps,))],
        spaces=(False, False),
    )
    from_core = lax.ppermute(part, "tp", core)
    w_k, hi_k, own = call(
        own_kernel,
        (tok_v, weight),
        [((depth, half), F32), ((depth, half), BF16), ((rows, half), F32)],
        [dma((steps,))],
        spaces=(True, False),
    )
    chip0, chip1 = call(chip_sum_kernel, (own, from_core), [keys16, keys16])
    from_chip0 = lax.ppermute(chip0, "tp", chip)
    from_chip1 = lax.ppermute(chip1, "tp", chip)
    left_vec = lax.ppermute(vec, "loop", right)
    proj0, tok_t = call(
        shadow_kernel,
        (tok_v, w_k, w_s, vec, left_vec, chip1),
        [((n, depth), F32), ((depth, rows), BF16)],
    )

    def norm(i, chip_part, from_chip, on_keys, gain_part, after):
        return call(
            functools.partial(norm_kernel, scale, i),
            (chip_part, from_chip, cotangent, gain, vec, left_vec, on_keys, gain_part, after),
            [keys16, ((n, rows), F32), (gain.shape, F32), (after.shape, after.dtype)],
            aliases={8: 3},
            nbytes=40 * MIB,
        )

    def step(i, kg, w):
        return call(
            functools.partial(step_kernel, rate, i),
            (tok_t, kg, w),
            [block, block16, block16, keys16],
            aliases={1: 3},
        )

    kg_k0, on_keys, gain_part, proj0 = norm(
        0, chip0, from_chip0, jnp.zeros((n, rows), F32), jnp.zeros(gain.shape, F32), proj0
    )
    kg_k1, on_keys, gain_part, kg_k0 = norm(1, chip1, from_chip1, on_keys, gain_part, kg_k0)
    on_keys_s = lax.ppermute(on_keys, "tp", core)
    s_k0, s_hi_k0, s_lo_k0, kg_k0 = step(0, kg_k0, w_k)
    s_k1, s_hi_k1, s_lo_k1, kg_k1 = step(1, kg_k1, w_k)
    first, second, proj, kg_k0, kg_k1 = call(
        functools.partial(project_kernel, rate),
        (on_keys, on_keys_s, proj0, tok_v, kg_k0, kg_k1),
        [((rank, depth), F32), ((rank, depth), F32), ((n, depth), F32), keys16, keys16],
        aliases={4: 3, 5: 4},
    )
    kg_s0 = lax.ppermute(kg_k0, "tp", core)
    kg_s1 = lax.ppermute(kg_k1, "tp", core)
    got_first = lax.ppermute(first, "loop", odd_edges)
    got_second = lax.ppermute(second, "loop", even_edges)
    s_s0, s_hi_s0, s_lo_s0, kg_s0 = step(0, kg_s0, w_s)
    s_s1, s_hi_s1, s_lo_s1, kg_s1 = step(1, kg_s1, w_s)
    edge_rows, gram = call(
        rows_kernel, (proj, got_first, got_second, s_lo_s0, s_lo_s1), [((n, depth), F32), ((n, 128), F32)]
    )
    (payload,) = call(
        back_kernel,
        (edge_rows, gram, gain_part, s_hi_k0, s_lo_k0, s_hi_k1, s_lo_k1, s_hi_s0, s_lo_s0, s_hi_s1, s_lo_s1),
        [((n, width + 256), F32)],
    )
    other_core = lax.ppermute(payload, "tp", core)
    pair, gain_grad = call(pair_kernel, (payload, other_core), [((n, width + 128), F32), (gain.shape, F32)])
    other_chip = lax.ppermute(pair, "tp", chip)
    aside, keep, gram = call(
        sum_kernel, (pair, other_chip), [((rank, width), F32), ((rank, width), F32), ((n, 128), F32)]
    )
    got = lax.ppermute(aside, ("loop", "tp"), along)
    inverse, lhs, new_gain = call(
        functools.partial(whiten_kernel, rank),
        (gram, edge_rows, gain, gain_grad),
        [((n, 128), F32), ((depth, 4 * n), BF16), (gain.shape, F32)],
        [pltpu.VMEM(gain.shape, F32), dma],
        out_spaces=(True, True, False),
    )
    (input_grad,) = call(
        functools.partial(input_kernel, scale),
        (kg_k0, kg_k1, kg_s0, kg_s1, hi_k, hi_s, keep),
        [((rows, depth), BF16)],
        [pltpu.VMEM((rows, depth), BF16), dma((steps,))],
        out_spaces=(False,),
    )
    (mine,) = call(
        edge_kernel, (keep, got, inverse, input_grad), [((rank, width), F32)], spaces=(True, True, True, False)
    )
    other = lax.ppermute(mine, "tp", core)
    parts = 5
    new_weights, new_vec = call(
        mix_kernel,
        (s_k0, s_k1, s_s0, s_s1, inverse, lhs, mine, other),
        [((depth, width), F32), ((rank, width), F32)],
        [
            pltpu.VMEM((depth, width), F32),
            pltpu.VMEM((rank, width), F32),
            pltpu.VMEM((4 * n, width), BF16),
            dma((parts,)),
            dma,
        ],
        out_spaces=(False, False),
    )
    return (new_weights[None], input_grad, new_gain, new_vec[None])


def solution(mesh):
    return jax.shard_map(
        shards,
        mesh=mesh,
        in_specs=(
            P("loop", "tp"),
            P("loop", "tp", None),
            P("loop", None),
            P("loop", None),
            P("loop", None, None),
        ),
        out_specs=(P("loop", "tp", None), P("loop", "tp"), P("loop", None), P("loop", None, None)),
        check_vma=False,
    )
```

```python
import functools

import jax
import jax.numpy as jnp
from jax import lax
from jax.experimental import pallas as pl
from jax.experimental.pallas import tpu as pltpu
from jax.sharding import PartitionSpec as P

F32 = jnp.float32
BF16 = jnp.bfloat16
MIB = 1024 * 1024
VM = pl.BlockSpec(memory_space=pltpu.VMEM)
ANY = pl.BlockSpec(memory_space=pl.ANY)
NT = (((1,), (1,)), ((), ()))


def in_vmem(x):
    return pltpu.with_memory_space_constraint(x, pltpu.VMEM)


def in_hbm(x):
    return pltpu.with_memory_space_constraint(x, pltpu.HBM)


def call(body, args, outs, scratch=(), limit=24, nbytes=1, spaces=None, out_spaces=None, aliases=None):
    spaces = spaces or (True,) * len(args)
    out_spaces = out_spaces or (True,) * len(outs)
    return pl.pallas_call(
        body,
        out_shape=[
            pltpu.VMEM(shape, dtype) if inside else pltpu.HBM(shape, dtype)
            for (shape, dtype), inside in zip(outs, out_spaces)
        ],
        in_specs=[VM if inside else ANY for inside in spaces],
        out_specs=[VM if inside else ANY for inside in out_spaces],
        scratch_shapes=list(scratch),
        input_output_aliases=aliases or {},
        compiler_params=pltpu.CompilerParams(vmem_limit_bytes=limit * MIB),
        cost_estimate=pl.CostEstimate(flops=400 * nbytes, bytes_accessed=nbytes, transcendentals=0),
    )(*[in_vmem(a) if inside else in_hbm(a) for a, inside in zip(args, spaces)])


def dot(a, b, dims=(((1,), (0,)), ((), ()))):
    return lax.dot_general(a, b, dims, preferred_element_type=F32)


def split(x):
    hi = x.astype(BF16)
    return hi, (x - hi.astype(F32)).astype(BF16)


def core_index():
    return lax.rem(lax.axis_index("tp"), 2)


def chunk_at(kept, i, wide):
    c = core_index()
    which = c if kept else 1 - c
    return pl.ds(pl.multiple_of(which * (2 * wide) + i * wide, 128), wide)


def half_in(w, to, kept, sems):
    half = to.shape[1]
    steps = sems.shape[0]
    k = to.shape[0] // steps
    c = core_index()
    cols = pl.ds(pl.multiple_of((c if kept else 1 - c) * half, 128), half)
    copies = []
    for j in range(steps):
        at = pl.ds(j * k, k)
        copies.append(pltpu.make_async_copy(w.at[at, cols], to.at[at], sems.at[j]))
        copies[j].start()
    return copies


def partial(tok_v, w_v, hi_v, copies):
    steps = len(copies)
    k = w_v.shape[0] // steps
    acc = None
    for j in range(steps):
        copies[j].wait()
        at = slice(j * k, (j + 1) * k)
        hi = w_v[at].astype(BF16)
        hi_v[at] = hi
        term = dot(tok_v[:, at], hi)
        acc = term if acc is None else acc + term
    return acc


def first_kernel(tok, w, tok_v, w_s, hi_s, part, tok_sem, w_sem):
    tok_copy = pltpu.make_async_copy(tok, tok_v, tok_sem)
    tok_copy.start()
    copies = half_in(w, w_s, False, w_sem)
    tok_copy.wait()
    part[...] = partial(tok_v, w_s, hi_s, copies).astype(BF16)


def own_kernel(tok_v, w, w_k, hi_k, own, w_sem):
    own[...] = partial(tok_v, w_k, hi_k, half_in(w, w_k, True, w_sem))


def chip_sum_kernel(own, got, out0, out1):
    wide = out0.shape[1]
    out0[...] = (own[:, :wide] + got[:, :wide].astype(F32)).astype(BF16)
    out1[...] = (own[:, wide:] + got[:, wide:].astype(F32)).astype(BF16)


def halves_of(vec, left_vec, at):
    hi, lo = split(jnp.concatenate([vec[:, at], left_vec[:, at]], axis=0))
    return jnp.concatenate([hi, lo], axis=0)


def shadow_kernel(tok_v, w_k, w_s, vec, left_vec, _, proj, tok_t):
    wide = w_k.shape[1] // 2
    n = proj.shape[0]
    total = None
    for w, kept, i in ((w_k, True, 0), (w_k, True, 1), (w_s, False, 0), (w_s, False, 1)):
        q = halves_of(vec, left_vec, chunk_at(kept, i, wide))
        w_hi, w_lo = split(w[:, i * wide : (i + 1) * wide])
        both = dot(q, w_hi, NT)
        term = both[:n] + both[n:] + dot(q[:n], w_lo, NT)
        total = term if total is None else total + term
    proj[...] = total
    tok_t[...] = tok_v[...].T


def norm_kernel(scale, i, own, got, cot, gain, vec, left_vec, on_keys_in, gain_in, _, kg, on_keys, gain_grad, passed):
    head = gain.shape[1]
    wide = own.shape[1]
    n = on_keys.shape[0]
    g = gain[...]
    start = chunk_at(True, i, wide).start
    total = gain_in[...]
    for h in range(wide // head):
        cols = slice(h * head, (h + 1) * head)
        keys = (own[:, cols].astype(F32) + got[:, cols].astype(F32)) * scale
        up = cot[:, pl.ds(pl.multiple_of(start + h * head, head), head)].astype(F32)
        gh = up * g
        inv = lax.rsqrt(jnp.mean(keys * keys, axis=-1, keepdims=True) + 1e-6)
        along = jnp.mean(gh * keys, axis=-1, keepdims=True)
        unit = keys * inv
        kg[:, cols] = (inv * (gh - unit * (inv * along))).astype(BF16)
        total = total + jnp.sum(up * unit, axis=0, keepdims=True)
    gain_grad[...] = total
    both = dot(halves_of(vec, left_vec, chunk_at(True, i, wide)), kg[...], NT)
    on_keys[...] = on_keys_in[...] + both[:n] + both[n:]


def odd_replica():
    return lax.rem(lax.axis_index("loop"), 2) == 1


def project_kernel(rate, mine, other, proj0, tok_v, first, second, out):
    hi, lo = split(mine[...] + other[...])
    rank = first.shape[0]
    n = 2 * rank
    both = dot(jnp.concatenate([hi, lo], axis=0), tok_v[...])
    proj = proj0[...] - rate * (both[:n] + both[n:])
    out[...] = proj
    odd = odd_replica()
    first[...] = jnp.where(odd, proj[:rank], proj[rank:])
    second[...] = jnp.where(odd, proj[rank:], proj[:rank])


def step_kernel(rate, i, tok_t, kg, w, out, out_hi, out_lo):
    wide = kg.shape[1]
    stepped = w[:, i * wide : (i + 1) * wide] - rate * dot(tok_t[...], kg[...])
    out[...] = stepped
    hi, lo = split(stepped)
    out_hi[...] = hi
    out_lo[...] = lo


def input_kernel(scale, kg_k0, kg_k1, kg_s0, kg_s1, hi_k, hi_s, _, out, stage, sem):
    wide = kg_k0.shape[1]
    steps = sem.shape[0]
    k = stage.shape[1] // steps
    copies = []
    for j in range(steps):
        at = slice(j * k, (j + 1) * k)
        total = None
        for kg, hi, i in ((kg_k0, hi_k, 0), (kg_k1, hi_k, 1), (kg_s0, hi_s, 0), (kg_s1, hi_s, 1)):
            term = dot(kg[...], hi[at, i * wide : (i + 1) * wide], NT)
            total = term if total is None else total + term
        stage[:, at] = (total * scale).astype(BF16)
        copies.append(pltpu.make_async_copy(stage.at[:, pl.ds(j * k, k)], out.at[:, pl.ds(j * k, k)], sem.at[j]))
        copies[j].start()
    for j in range(steps):
        copies[j].wait()


def rows_kernel(proj, got_first, got_second, _0, _1, _2, _3, rows_out, gram_out):
    n = proj.shape[0]
    rank = n // 2
    odd = odd_replica()
    got_right = jnp.where(odd, got_first[...], got_second[...])
    got_left = jnp.where(odd, got_second[...], got_first[...])
    rows = jnp.concatenate([proj[:rank] - got_right, got_left - proj[rank:]], axis=0)
    rows_out[...] = rows
    gram = lax.dot_general(rows, rows, NT, precision=lax.Precision.HIGHEST, preferred_element_type=F32)
    gram_out[...] = jnp.concatenate([gram, jnp.zeros((n, 128 - n), F32)], axis=1)


def back_kernel(rows, gram, gain_grad, *refs):
    *blocks, out = refs
    wide = blocks[0].shape[1]
    width = 4 * wide
    n = rows.shape[0]
    r_hi, r_lo = split(rows[...])
    r = jnp.concatenate([r_hi, r_lo], axis=0)
    for j, (kept, i) in enumerate(((True, 0), (True, 1), (False, 0), (False, 1))):
        s_hi, s_lo = blocks[2 * j], blocks[2 * j + 1]
        both = dot(r, s_hi[...])
        out[:, chunk_at(kept, i, wide)] = both[:n] + both[n:] + dot(r_hi, s_lo[...])
    out[:, width : width + 128] = gram[...]
    out[:, width + 128 :] = jnp.broadcast_to(gain_grad[...], (n, 128))


def pair_kernel(mine, other, pair, aside, gain_grad):
    rank, width = aside.shape
    both = mine[...] + other[...]
    pair[...] = both[:, : width + 128]
    aside[...] = jnp.where(core_index() == 0, both[:rank, :width], both[rank:, :width])
    gain_grad[...] = both[0:1, width + 128 :]


def edge_kernel(pair, other, near, far, _, out, gram):
    rank, width = out.shape
    whole = pair[...] + other[...]
    beyond = near[...] + far[...]
    out[...] = jnp.where(core_index() == 0, beyond - whole[rank:, :width], whole[:rank, :width] - beyond)
    gram[...] = whole[:, width:]


def inverse_factor(gram, rank):
    n = gram.shape[0]
    width = gram.shape[1]
    lane = lax.broadcasted_iota(jnp.int32, (rank, width), 1)
    row = lax.broadcasted_iota(jnp.int32, (rank, width), 0)
    parts = []
    for e in range(n // rank):
        a = gram[e * rank : (e + 1) * rank]
        a = jnp.where((lane >= e * rank) & (lane < (e + 1) * rank), a, 0.0)
        a = jnp.where(lane == n + e * rank + row, 1.0, a)
        for i in range(rank):
            col = a[:, e * rank + i : e * rank + i + 1]
            pivot = lax.rsqrt(col[i : i + 1])
            line = a[i : i + 1] * pivot
            a = jnp.where(row == i, line, jnp.where(row > i, a - (col * pivot) * line, a))
        parts.append(a)
    return jnp.concatenate(parts, axis=0)


def apply_inverse(both, x, n):
    total = None
    for j in range(n):
        term = both[:, n + j : n + j + 1] * x[j : j + 1]
        total = term if total is None else total + term
    return total


def whiten_kernel(rank, gram, rows, gain, gain_grad, inverse, lhs, new_gain, stage, sem):
    stage[...] = gain[...] - 0.002 * gain_grad[...]
    copy = pltpu.make_async_copy(stage, new_gain, sem)
    copy.start()
    both = inverse_factor(gram[...], rank)
    inverse[...] = both
    u_hi, u_lo = split(apply_inverse(both, rows[...], 2 * rank))
    lhs[...] = jnp.concatenate([u_hi, u_hi, u_lo, jnp.zeros_like(u_hi)], axis=0).T
    copy.wait()


def mix_kernel(s_k0, s_k1, s_s0, s_s1, inverse, lhs, mine, other, out, new_vec, stage, vec_stage, right_side, sem, vec_sem):
    rank, width = vec_stage.shape
    depth, wide = s_k0.shape
    n = 2 * rank
    first = core_index() == 0
    a, b = mine[...], other[...]
    back = jnp.concatenate([jnp.where(first, b, a), jnp.where(first, a, b)], axis=0)
    nv = apply_inverse(inverse[...], back, n)
    sign = jnp.where(lax.broadcasted_iota(jnp.int32, (n, width), 0) < rank, 1.0 / 3.0, -1.0 / 3.0)
    v_hi, v_lo = split(nv * sign)
    right_side[...] = jnp.concatenate([v_hi, v_lo, v_hi, jnp.zeros_like(v_hi)], axis=0)
    vec_stage[...] = nv[:rank]
    vec_copy = pltpu.make_async_copy(vec_stage, new_vec, vec_sem)
    vec_copy.start()
    parts = sem.shape[0]
    k = depth // parts
    copies = []
    for p in range(parts):
        at = slice(p * k, (p + 1) * k)
        for s, kept, i in ((s_k0, True, 0), (s_k1, True, 1), (s_s0, False, 0), (s_s1, False, 1)):
            cols = chunk_at(kept, i, wide)
            stage[at, cols] = s[at] - dot(lhs[at], right_side[:, cols])
        copies.append(pltpu.make_async_copy(stage.at[pl.ds(p * k, k)], out.at[pl.ds(p * k, k)], sem.at[p]))
        copies[p].start()
    for copy in copies:
        copy.wait()
    vec_copy.wait()


def shards(tokens, weights, gain, cotangent, vectors):
    rows, depth = tokens.shape
    width = weights.shape[2]
    half = width // 2
    wide = half // 2
    rank = vectors.shape[1]
    n = 2 * rank
    tp = lax.axis_size("tp")
    loop = lax.axis_size("loop")
    scale = (depth * tp) ** -0.5
    rate = 0.1 * scale
    weight = weights[0]
    vec = vectors[0]
    core = [(i, i ^ 1) for i in range(tp)]
    chip = [(i, i ^ 2) for i in range(tp)]
    right = [(i, (i + 1) % loop) for i in range(loop)]
    odd_edges = [(i, (i + 1 if i % 2 else i - 1) % loop) for i in range(loop)]
    even_edges = [(i, i ^ 1) for i in range(loop)]
    along = [
        (i * tp + t, ((i + 1) % loop if t % 2 == 0 else (i - 1) % loop) * tp + t) for i in range(loop) for t in range(tp)
    ]
    along_far = [(i, j ^ 2) for i, j in along]
    dma = pltpu.SemaphoreType.DMA
    block, block16, keys16 = ((depth, wide), F32), ((depth, wide), BF16), ((rows, wide), BF16)
    steps = 5

    tok_v, w_s, hi_s, part = call(
        first_kernel,
        (tokens, weight),
        [((rows, depth), BF16), ((depth, half), F32), ((depth, half), BF16), ((rows, half), BF16)],
        [dma, dma((steps,))],
        spaces=(False, False),
    )
    from_core = lax.ppermute(part, "tp", core)
    w_k, hi_k, own = call(
        own_kernel,
        (tok_v, weight),
        [((depth, half), F32), ((depth, half), BF16), ((rows, half), F32)],
        [dma((steps,))],
        spaces=(True, False),
    )
    chip0, chip1 = call(chip_sum_kernel, (own, from_core), [keys16, keys16])
    from_chip0 = lax.ppermute(chip0, "tp", chip)
    from_chip1 = lax.ppermute(chip1, "tp", chip)
    left_vec = lax.ppermute(vec, "loop", right)
    proj0, tok_t = call(
        shadow_kernel,
        (tok_v, w_k, w_s, vec, left_vec, chip1),
        [((n, depth), F32), ((depth, rows), BF16)],
    )

    def norm(i, chip_part, from_chip, on_keys, gain_part, after):
        return call(
            functools.partial(norm_kernel, scale, i),
            (chip_part, from_chip, cotangent, gain, vec, left_vec, on_keys, gain_part, after),
            [keys16, ((n, rows), F32), (gain.shape, F32), (after.shape, after.dtype)],
            aliases={8: 3},
            nbytes=40 * MIB if i == 0 else 1,
        )

    def step(i, kg, w):
        return call(
            functools.partial(step_kernel, rate, i),
            (tok_t, kg, w),
            [block, block16, block16],
        )

    kg_k0, on_keys, gain_part, proj0 = norm(
        0, chip0, from_chip0, jnp.zeros((n, rows), F32), jnp.zeros(gain.shape, F32), proj0
    )
    kg_k1, on_keys, gain_part, kg_k0 = norm(1, chip1, from_chip1, on_keys, gain_part, kg_k0)
    on_keys_s = lax.ppermute(on_keys, "tp", core)
    s_k0, s_hi_k0, s_lo_k0 = step(0, kg_k0, w_k)
    s_k1, s_hi_k1, s_lo_k1 = step(1, kg_k1, w_k)
    kg_s0 = lax.ppermute(kg_k0, "tp", core)
    kg_s1 = lax.ppermute(kg_k1, "tp", core)
    first, second, proj = call(
        functools.partial(project_kernel, rate),
        (on_keys, on_keys_s, proj0, tok_v),
        [((rank, depth), F32), ((rank, depth), F32), ((n, depth), F32)],
        nbytes=40 * MIB,
    )
    got_first = lax.ppermute(first, "loop", odd_edges)
    got_second = lax.ppermute(second, "loop", even_edges)
    s_s0, s_hi_s0, s_lo_s0 = step(0, kg_s0, w_s)
    s_s1, s_hi_s1, s_lo_s1 = step(1, kg_s1, w_s)
    edge_rows, gram = call(
        rows_kernel,
        (proj, got_first, got_second, s_lo_k0, s_lo_k1, s_lo_s0, s_lo_s1),
        [((n, depth), F32), ((n, 128), F32)],
    )
    (payload,) = call(
        back_kernel,
        (edge_rows, gram, gain_part, s_hi_k0, s_lo_k0, s_hi_k1, s_lo_k1, s_hi_s0, s_lo_s0, s_hi_s1, s_lo_s1),
        [((n, width + 256), F32)],
    )
    other_core = lax.ppermute(payload, "tp", core)
    pair, aside, gain_grad = call(
        pair_kernel,
        (payload, other_core),
        [((n, width + 128), F32), ((rank, width), F32), (gain.shape, F32)],
    )
    everyone = ("loop", "tp")
    near = lax.ppermute(aside, everyone, along)
    far = lax.ppermute(aside, everyone, along_far)
    other_chip = lax.ppermute(pair, "tp", chip)
    (input_grad,) = call(
        functools.partial(input_kernel, scale),
        (kg_k0, kg_k1, kg_s0, kg_s1, hi_k, hi_s, aside),
        [((rows, depth), BF16)],
        [pltpu.VMEM((rows, depth), BF16), dma((steps,))],
        out_spaces=(False,),
    )
    mine, gram = call(
        edge_kernel,
        (pair, other_chip, near, far, input_grad),
        [((rank, width), F32), ((n, 128), F32)],
        spaces=(True, True, True, True, False),
    )
    other = lax.ppermute(mine, "tp", core)
    inverse, lhs, new_gain = call(
        functools.partial(whiten_kernel, rank),
        (gram, edge_rows, gain, gain_grad),
        [((n, 128), F32), ((depth, 4 * n), BF16), (gain.shape, F32)],
        [pltpu.VMEM(gain.shape, F32), dma],
        out_spaces=(True, True, False),
    )
    parts = 10
    new_weights, new_vec = call(
        mix_kernel,
        (s_k0, s_k1, s_s0, s_s1, inverse, lhs, mine, other),
        [((depth, width), F32), ((rank, width), F32)],
        [
            pltpu.VMEM((depth, width), F32),
            pltpu.VMEM((rank, width), F32),
            pltpu.VMEM((4 * n, width), BF16),
            dma((parts,)),
            dma,
        ],
        out_spaces=(False, False),
    )
    return (new_weights[None], input_grad, new_gain, new_vec[None])


def solution(mesh):
    return jax.shard_map(
        shards,
        mesh=mesh,
        in_specs=(
            P("loop", "tp"),
            P("loop", "tp", None),
            P("loop", None),
            P("loop", None),
            P("loop", None, None),
        ),
        out_specs=(P("loop", "tp", None), P("loop", "tp"), P("loop", None), P("loop", None, None)),
        check_vma=False,
    )
```

```python
import functools

import jax
import jax.numpy as jnp
from jax import lax
from jax.experimental import pallas as pl
from jax.experimental.pallas import tpu as pltpu
from jax.sharding import PartitionSpec as P

F32 = jnp.float32
BF16 = jnp.bfloat16
MIB = 1024 * 1024
VM = pl.BlockSpec(memory_space=pltpu.VMEM)
ANY = pl.BlockSpec(memory_space=pl.ANY)
NT = (((1,), (1,)), ((), ()))


def in_vmem(x):
    return pltpu.with_memory_space_constraint(x, pltpu.VMEM)


def in_hbm(x):
    return pltpu.with_memory_space_constraint(x, pltpu.HBM)


def call(body, args, outs, scratch=(), limit=24, nbytes=1, spaces=None, out_spaces=None, aliases=None):
    spaces = spaces or (True,) * len(args)
    out_spaces = out_spaces or (True,) * len(outs)
    return pl.pallas_call(
        body,
        out_shape=[
            pltpu.VMEM(shape, dtype) if inside else pltpu.HBM(shape, dtype)
            for (shape, dtype), inside in zip(outs, out_spaces)
        ],
        in_specs=[VM if inside else ANY for inside in spaces],
        out_specs=[VM if inside else ANY for inside in out_spaces],
        scratch_shapes=list(scratch),
        input_output_aliases=aliases or {},
        compiler_params=pltpu.CompilerParams(vmem_limit_bytes=limit * MIB),
        cost_estimate=pl.CostEstimate(flops=400 * nbytes, bytes_accessed=nbytes, transcendentals=0),
    )(*[in_vmem(a) if inside else in_hbm(a) for a, inside in zip(args, spaces)])


def dot(a, b, dims=(((1,), (0,)), ((), ()))):
    return lax.dot_general(a, b, dims, preferred_element_type=F32)


def split(x):
    hi = x.astype(BF16)
    return hi, (x - hi.astype(F32)).astype(BF16)


def core_index():
    return lax.rem(lax.axis_index("tp"), 2)


def chunk_at(kept, i, wide):
    c = core_index()
    which = c if kept else 1 - c
    return pl.ds(pl.multiple_of(which * (2 * wide) + i * wide, 128), wide)


def half_in(w, to, kept, sems):
    half = to.shape[1]
    steps = sems.shape[0]
    k = to.shape[0] // steps
    c = core_index()
    cols = pl.ds(pl.multiple_of((c if kept else 1 - c) * half, 128), half)
    copies = []
    for j in range(steps):
        at = pl.ds(j * k, k)
        copies.append(pltpu.make_async_copy(w.at[at, cols], to.at[at], sems.at[j]))
        copies[j].start()
    return copies


def partial(tok_v, w_v, hi_v, copies):
    steps = len(copies)
    k = w_v.shape[0] // steps
    acc = None
    for j in range(steps):
        copies[j].wait()
        at = slice(j * k, (j + 1) * k)
        hi = w_v[at].astype(BF16)
        hi_v[at] = hi
        term = dot(tok_v[:, at], hi)
        acc = term if acc is None else acc + term
    return acc


def first_kernel(tok, w, tok_v, w_s, hi_s, part, tok_sem, w_sem):
    tok_copy = pltpu.make_async_copy(tok, tok_v, tok_sem)
    tok_copy.start()
    copies = half_in(w, w_s, False, w_sem)
    tok_copy.wait()
    part[...] = partial(tok_v, w_s, hi_s, copies).astype(BF16)


def own_kernel(tok_v, w, w_k, hi_k, own, w_sem):
    own[...] = partial(tok_v, w_k, hi_k, half_in(w, w_k, True, w_sem))


def chip_sum_kernel(own, got, out0, out1):
    wide = out0.shape[1]
    out0[...] = (own[:, :wide] + got[:, :wide].astype(F32)).astype(BF16)
    out1[...] = (own[:, wide:] + got[:, wide:].astype(F32)).astype(BF16)


def halves_of(vec, left_vec, at):
    hi, lo = split(jnp.concatenate([vec[:, at], left_vec[:, at]], axis=0))
    return jnp.concatenate([hi, lo], axis=0)


def shadow_kernel(tok_v, w_k, w_s, vec, left_vec, _, proj, tok_t):
    wide = w_k.shape[1] // 2
    n = proj.shape[0]
    total = None
    for w, kept, i in ((w_k, True, 0), (w_k, True, 1), (w_s, False, 0), (w_s, False, 1)):
        q = halves_of(vec, left_vec, chunk_at(kept, i, wide))
        w_hi, w_lo = split(w[:, i * wide : (i + 1) * wide])
        both = dot(q, w_hi, NT)
        term = both[:n] + both[n:] + dot(q[:n], w_lo, NT)
        total = term if total is None else total + term
    proj[...] = total
    tok_t[...] = tok_v[...].T


def norm_kernel(scale, i, own, got, cot, gain, vec, left_vec, on_keys_in, gain_in, _, kg, on_keys, gain_grad, passed):
    head = gain.shape[1]
    wide = own.shape[1]
    n = on_keys.shape[0]
    g = gain[...]
    start = chunk_at(True, i, wide).start
    total = gain_in[...]
    for h in range(wide // head):
        cols = slice(h * head, (h + 1) * head)
        keys = (own[:, cols].astype(F32) + got[:, cols].astype(F32)) * scale
        up = cot[:, pl.ds(pl.multiple_of(start + h * head, head), head)].astype(F32)
        gh = up * g
        inv = lax.rsqrt(jnp.mean(keys * keys, axis=-1, keepdims=True) + 1e-6)
        along = jnp.mean(gh * keys, axis=-1, keepdims=True)
        unit = keys * inv
        kg[:, cols] = (inv * (gh - unit * (inv * along))).astype(BF16)
        total = total + jnp.sum(up * unit, axis=0, keepdims=True)
    gain_grad[...] = total
    both = dot(halves_of(vec, left_vec, chunk_at(True, i, wide)), kg[...], NT)
    on_keys[...] = on_keys_in[...] + both[:n] + both[n:]


def odd_replica():
    return lax.rem(lax.axis_index("loop"), 2) == 1


def project_kernel(rate, mine, other, proj0, tok_v, first, second, out):
    hi, lo = split(mine[...] + other[...])
    rank = first.shape[0]
    n = 2 * rank
    both = dot(jnp.concatenate([hi, lo], axis=0), tok_v[...])
    proj = proj0[...] - rate * (both[:n] + both[n:])
    out[...] = proj
    odd = odd_replica()
    first[...] = jnp.where(odd, proj[:rank], proj[rank:])
    second[...] = jnp.where(odd, proj[rank:], proj[:rank])


def step_kernel(rate, i, tok_t, kg, w, out, out_hi, out_lo):
    wide = kg.shape[1]
    stepped = w[:, i * wide : (i + 1) * wide] - rate * dot(tok_t[...], kg[...])
    out[...] = stepped
    hi, lo = split(stepped)
    out_hi[...] = hi
    out_lo[...] = lo


def input_kernel(scale, kg_k0, kg_k1, kg_s0, kg_s1, hi_k, hi_s, _, out, stage, sem):
    wide = kg_k0.shape[1]
    steps = sem.shape[0]
    k = stage.shape[1] // steps
    copies = []
    for j in range(steps):
        at = slice(j * k, (j + 1) * k)
        total = None
        for kg, hi, i in ((kg_k0, hi_k, 0), (kg_k1, hi_k, 1), (kg_s0, hi_s, 0), (kg_s1, hi_s, 1)):
            term = dot(kg[...], hi[at, i * wide : (i + 1) * wide], NT)
            total = term if total is None else total + term
        stage[:, at] = (total * scale).astype(BF16)
        copies.append(pltpu.make_async_copy(stage.at[:, pl.ds(j * k, k)], out.at[:, pl.ds(j * k, k)], sem.at[j]))
        copies[j].start()
    for j in range(steps):
        copies[j].wait()


def back_kernel(proj, got_first, got_second, gain_grad, *refs):
    *blocks, rows_out, out = refs
    wide = blocks[0].shape[1]
    width = 4 * wide
    n = proj.shape[0]
    rank = n // 2
    odd = odd_replica()
    got_right = jnp.where(odd, got_first[...], got_second[...])
    got_left = jnp.where(odd, got_second[...], got_first[...])
    rows = jnp.concatenate([proj[:rank] - got_right, got_left - proj[rank:]], axis=0)
    rows_out[...] = rows
    r_hi, r_lo = split(rows)
    r = jnp.concatenate([r_hi, r_lo], axis=0)
    for j, (kept, i) in enumerate(((True, 0), (True, 1), (False, 0), (False, 1))):
        s_hi, s_lo = blocks[2 * j], blocks[2 * j + 1]
        both = dot(r, s_hi[...])
        out[:, chunk_at(kept, i, wide)] = both[:n] + both[n:] + dot(r_hi, s_lo[...])
    square = dot(r, r, NT)
    gram = (square[:n, :n] + square[n:, n:]) + (square[:n, n:] + square[n:, :n])
    out[:, width : width + 128] = jnp.concatenate([gram, jnp.zeros((n, 128 - n), F32)], axis=1)
    out[:, width + 128 :] = jnp.broadcast_to(gain_grad[...], (n, 128))


def pair_kernel(mine, other, keep, aside, gain_grad):
    rank = keep.shape[0]
    width = mine.shape[1] - 256
    both = mine[...] + other[...]
    first = core_index() == 0
    keep[:, :width] = jnp.where(first, both[rank:, :width], both[:rank, :width])
    for e in range(2):
        keep[:, width + 128 * e : width + 128 * (e + 1)] = both[e * rank : (e + 1) * rank, width : width + 128]
    aside[:, :width] = jnp.where(first, both[:rank, :width], both[rank:, :width])
    aside[:, width:] = jnp.zeros((rank, aside.shape[1] - width), F32)
    gain_grad[...] = both[0:1, width + 128 :]


def edge_kernel(keep, other, near, far, _, out, gram):
    rank, width = out.shape
    whole = keep[...] + other[...]
    beyond = near[:, :width] + far[:, :width]
    out[...] = jnp.where(core_index() == 0, beyond - whole[:, :width], whole[:, :width] - beyond)
    for e in range(2):
        gram[e * rank : (e + 1) * rank] = whole[:, width + 128 * e : width + 128 * (e + 1)]


def inverse_factor(gram, rank):
    n = gram.shape[0]
    width = gram.shape[1]
    lane = lax.broadcasted_iota(jnp.int32, (rank, width), 1)
    row = lax.broadcasted_iota(jnp.int32, (rank, width), 0)
    parts = []
    for e in range(n // rank):
        a = gram[e * rank : (e + 1) * rank]
        a = jnp.where((lane >= e * rank) & (lane < (e + 1) * rank), a, 0.0)
        a = jnp.where(lane == n + e * rank + row, 1.0, a)
        for i in range(rank):
            col = a[:, e * rank + i : e * rank + i + 1]
            pivot = lax.rsqrt(col[i : i + 1])
            line = a[i : i + 1] * pivot
            a = jnp.where(row == i, line, jnp.where(row > i, a - (col * pivot) * line, a))
        parts.append(a)
    return jnp.concatenate(parts, axis=0)


def apply_inverse(both, x, n):
    total = None
    for j in range(n):
        term = both[:, n + j : n + j + 1] * x[j : j + 1]
        total = term if total is None else total + term
    return total


def whiten_kernel(rank, gram, rows, gain, gain_grad, inverse, lhs, new_gain, stage, sem):
    stage[...] = gain[...] - 0.002 * gain_grad[...]
    copy = pltpu.make_async_copy(stage, new_gain, sem)
    copy.start()
    both = inverse_factor(gram[...], rank)
    inverse[...] = both
    u_hi, u_lo = split(apply_inverse(both, rows[...], 2 * rank))
    lhs[...] = jnp.concatenate([u_hi, u_hi, u_lo, jnp.zeros_like(u_hi)], axis=0).T
    copy.wait()


def mix_kernel(s_k0, s_k1, s_s0, s_s1, inverse, lhs, mine, other, out, new_vec, stage, vec_stage, right_side, sem, vec_sem):
    rank, width = vec_stage.shape
    depth, wide = s_k0.shape
    n = 2 * rank
    first = core_index() == 0
    a, b = mine[...], other[...]
    back = jnp.concatenate([jnp.where(first, b, a), jnp.where(first, a, b)], axis=0)
    nv = apply_inverse(inverse[...], back, n)
    sign = jnp.where(lax.broadcasted_iota(jnp.int32, (n, width), 0) < rank, 1.0 / 3.0, -1.0 / 3.0)
    v_hi, v_lo = split(nv * sign)
    right_side[...] = jnp.concatenate([v_hi, v_lo, v_hi, jnp.zeros_like(v_hi)], axis=0)
    vec_stage[...] = nv[:rank]
    vec_copy = pltpu.make_async_copy(vec_stage, new_vec, vec_sem)
    vec_copy.start()
    parts = sem.shape[0]
    k = depth // parts
    copies = []
    for p in range(parts):
        at = slice(p * k, (p + 1) * k)
        for s, kept, i in ((s_k0, True, 0), (s_k1, True, 1), (s_s0, False, 0), (s_s1, False, 1)):
            cols = chunk_at(kept, i, wide)
            stage[at, cols] = s[at] - dot(lhs[at], right_side[:, cols])
        copies.append(pltpu.make_async_copy(stage.at[pl.ds(p * k, k)], out.at[pl.ds(p * k, k)], sem.at[p]))
        copies[p].start()
    for copy in copies:
        copy.wait()
    vec_copy.wait()


def shards(tokens, weights, gain, cotangent, vectors):
    rows, depth = tokens.shape
    width = weights.shape[2]
    half = width // 2
    wide = half // 2
    rank = vectors.shape[1]
    n = 2 * rank
    tp = lax.axis_size("tp")
    loop = lax.axis_size("loop")
    scale = (depth * tp) ** -0.5
    rate = 0.1 * scale
    weight = weights[0]
    vec = vectors[0]
    core = [(i, i ^ 1) for i in range(tp)]
    chip = [(i, i ^ 2) for i in range(tp)]
    right = [(i, (i + 1) % loop) for i in range(loop)]
    odd_edges = [(i, (i + 1 if i % 2 else i - 1) % loop) for i in range(loop)]
    even_edges = [(i, i ^ 1) for i in range(loop)]
    along = [
        (i * tp + t, ((i + 1) % loop if t % 2 == 0 else (i - 1) % loop) * tp + t) for i in range(loop) for t in range(tp)
    ]
    along_far = [(i, j ^ 2) for i, j in along]
    dma = pltpu.SemaphoreType.DMA
    block, block16, keys16 = ((depth, wide), F32), ((depth, wide), BF16), ((rows, wide), BF16)
    steps = 5

    tok_v, w_s, hi_s, part = call(
        first_kernel,
        (tokens, weight),
        [((rows, depth), BF16), ((depth, half), F32), ((depth, half), BF16), ((rows, half), BF16)],
        [dma, dma((steps,))],
        spaces=(False, False),
    )
    from_core = lax.ppermute(part, "tp", core)
    w_k, hi_k, own = call(
        own_kernel,
        (tok_v, weight),
        [((depth, half), F32), ((depth, half), BF16), ((rows, half), F32)],
        [dma((steps,))],
        spaces=(True, False),
    )
    chip0, chip1 = call(chip_sum_kernel, (own, from_core), [keys16, keys16])
    from_chip0 = lax.ppermute(chip0, "tp", chip)
    from_chip1 = lax.ppermute(chip1, "tp", chip)
    left_vec = lax.ppermute(vec, "loop", right)
    proj0, tok_t = call(
        shadow_kernel,
        (tok_v, w_k, w_s, vec, left_vec, chip1),
        [((n, depth), F32), ((depth, rows), BF16)],
    )

    def norm(i, chip_part, from_chip, on_keys, gain_part, after):
        return call(
            functools.partial(norm_kernel, scale, i),
            (chip_part, from_chip, cotangent, gain, vec, left_vec, on_keys, gain_part, after),
            [keys16, ((n, rows), F32), (gain.shape, F32), (after.shape, after.dtype)],
            aliases={8: 3},
            nbytes=40 * MIB if i == 0 else 1,
        )

    def step(i, kg, w):
        return call(
            functools.partial(step_kernel, rate, i),
            (tok_t, kg, w),
            [block, block16, block16],
        )

    kg_k0, on_keys, gain_part, proj0 = norm(
        0, chip0, from_chip0, jnp.zeros((n, rows), F32), jnp.zeros(gain.shape, F32), proj0
    )
    kg_k1, on_keys, gain_part, kg_k0 = norm(1, chip1, from_chip1, on_keys, gain_part, kg_k0)
    on_keys_s = lax.ppermute(on_keys, "tp", core)
    s_k0, s_hi_k0, s_lo_k0 = step(0, kg_k0, w_k)
    s_k1, s_hi_k1, s_lo_k1 = step(1, kg_k1, w_k)
    kg_s0 = lax.ppermute(kg_k0, "tp", core)
    kg_s1 = lax.ppermute(kg_k1, "tp", core)
    first, second, proj = call(
        functools.partial(project_kernel, rate),
        (on_keys, on_keys_s, proj0, tok_v),
        [((rank, depth), F32), ((rank, depth), F32), ((n, depth), F32)],
        nbytes=40 * MIB,
    )
    got_first = lax.ppermute(first, "loop", odd_edges)
    got_second = lax.ppermute(second, "loop", even_edges)
    s_s0, s_hi_s0, s_lo_s0 = step(0, kg_s0, w_s)
    s_s1, s_hi_s1, s_lo_s1 = step(1, kg_s1, w_s)
    edge_rows, payload = call(
        back_kernel,
        (proj, got_first, got_second, gain_part)
        + (s_hi_k0, s_lo_k0, s_hi_k1, s_lo_k1, s_hi_s0, s_lo_s0, s_hi_s1, s_lo_s1),
        [((n, depth), F32), ((n, width + 256), F32)],
    )
    other_core = lax.ppermute(payload, "tp", core)
    keep, aside, gain_grad = call(
        pair_kernel,
        (payload, other_core),
        [((rank, width + 256), F32), ((rank, width + 384), F32), (gain.shape, F32)],
    )
    everyone = ("loop", "tp")
    far = lax.ppermute(aside, everyone, along_far)
    near = lax.ppermute(aside, everyone, along)
    other_chip = lax.ppermute(keep, "tp", chip)
    (input_grad,) = call(
        functools.partial(input_kernel, scale),
        (kg_k0, kg_k1, kg_s0, kg_s1, hi_k, hi_s, aside),
        [((rows, depth), BF16)],
        [pltpu.VMEM((rows, depth), BF16), dma((steps,))],
        out_spaces=(False,),
    )
    mine, gram = call(
        edge_kernel,
        (keep, other_chip, near, far, input_grad),
        [((rank, width), F32), ((n, 128), F32)],
        spaces=(True, True, True, True, False),
    )
    other = lax.ppermute(mine, "tp", core)
    inverse, lhs, new_gain = call(
        functools.partial(whiten_kernel, rank),
        (gram, edge_rows, gain, gain_grad),
        [((n, 128), F32), ((depth, 4 * n), BF16), (gain.shape, F32)],
        [pltpu.VMEM(gain.shape, F32), dma],
        out_spaces=(True, True, False),
    )
    parts = 10
    new_weights, new_vec = call(
        mix_kernel,
        (s_k0, s_k1, s_s0, s_s1, inverse, lhs, mine, other),
        [((depth, width), F32), ((rank, width), F32)],
        [
            pltpu.VMEM((depth, width), F32),
            pltpu.VMEM((rank, width), F32),
            pltpu.VMEM((4 * n, width), BF16),
            dma((parts,)),
            dma,
        ],
        out_spaces=(False, False),
    )
    return (new_weights[None], input_grad, new_gain, new_vec[None])


def solution(mesh):
    return jax.shard_map(
        shards,
        mesh=mesh,
        in_specs=(
            P("loop", "tp"),
            P("loop", "tp", None),
            P("loop", None),
            P("loop", None),
            P("loop", None, None),
        ),
        out_specs=(P("loop", "tp", None), P("loop", "tp"), P("loop", None), P("loop", None, None)),
        check_vma=False,
    )
```

```python
import functools

import jax
import jax.numpy as jnp
from jax import lax
from jax.experimental import pallas as pl
from jax.experimental.pallas import tpu as pltpu
from jax.sharding import PartitionSpec as P

F32 = jnp.float32
BF16 = jnp.bfloat16
MIB = 1024 * 1024
VM = pl.BlockSpec(memory_space=pltpu.VMEM)
ANY = pl.BlockSpec(memory_space=pl.ANY)
NT = (((1,), (1,)), ((), ()))


def in_vmem(x):
    return pltpu.with_memory_space_constraint(x, pltpu.VMEM)


def in_hbm(x):
    return pltpu.with_memory_space_constraint(x, pltpu.HBM)


def call(body, args, outs, scratch=(), limit=24, nbytes=1, spaces=None, out_spaces=None, aliases=None):
    spaces = spaces or (True,) * len(args)
    out_spaces = out_spaces or (True,) * len(outs)
    return pl.pallas_call(
        body,
        out_shape=[
            pltpu.VMEM(shape, dtype) if inside else pltpu.HBM(shape, dtype)
            for (shape, dtype), inside in zip(outs, out_spaces)
        ],
        in_specs=[VM if inside else ANY for inside in spaces],
        out_specs=[VM if inside else ANY for inside in out_spaces],
        scratch_shapes=list(scratch),
        input_output_aliases=aliases or {},
        compiler_params=pltpu.CompilerParams(vmem_limit_bytes=limit * MIB),
        cost_estimate=pl.CostEstimate(flops=400 * nbytes, bytes_accessed=nbytes, transcendentals=0),
    )(*[in_vmem(a) if inside else in_hbm(a) for a, inside in zip(args, spaces)])


def dot(a, b, dims=(((1,), (0,)), ((), ()))):
    return lax.dot_general(a, b, dims, preferred_element_type=F32)


def split(x):
    hi = x.astype(BF16)
    return hi, (x - hi.astype(F32)).astype(BF16)


def core_index():
    return lax.rem(lax.axis_index("tp"), 2)


def chunk_at(kept, i, wide):
    c = core_index()
    which = c if kept else 1 - c
    return pl.ds(pl.multiple_of(which * (2 * wide) + i * wide, 128), wide)


def half_in(w, to, kept, sems):
    half = to.shape[1]
    steps = sems.shape[0]
    k = to.shape[0] // steps
    c = core_index()
    cols = pl.ds(pl.multiple_of((c if kept else 1 - c) * half, 128), half)
    copies = []
    for j in range(steps):
        at = pl.ds(j * k, k)
        copies.append(pltpu.make_async_copy(w.at[at, cols], to.at[at], sems.at[j]))
        copies[j].start()
    return copies


def partial(tok_v, w_v, hi_v, copies):
    steps = len(copies)
    k = w_v.shape[0] // steps
    acc = None
    for j in range(steps):
        copies[j].wait()
        at = slice(j * k, (j + 1) * k)
        hi = w_v[at].astype(BF16)
        hi_v[at] = hi
        term = dot(tok_v[:, at], hi)
        acc = term if acc is None else acc + term
    return acc


def first_kernel(tok, w, tok_v, w_s, hi_s, part, tok_sem, w_sem):
    tok_copy = pltpu.make_async_copy(tok, tok_v, tok_sem)
    tok_copy.start()
    copies = half_in(w, w_s, False, w_sem)
    tok_copy.wait()
    part[...] = partial(tok_v, w_s, hi_s, copies).astype(BF16)


def own_kernel(tok_v, w, w_k, hi_k, own, w_sem):
    own[...] = partial(tok_v, w_k, hi_k, half_in(w, w_k, True, w_sem))


def chip_sum_kernel(own, got, out0, out1):
    wide = out0.shape[1]
    out0[...] = (own[:, :wide] + got[:, :wide].astype(F32)).astype(BF16)
    out1[...] = (own[:, wide:] + got[:, wide:].astype(F32)).astype(BF16)


def halves_of(vec, left_vec, at):
    hi, lo = split(jnp.concatenate([vec[:, at], left_vec[:, at]], axis=0))
    return jnp.concatenate([hi, lo], axis=0)


def shadow_kernel(tok_v, w_k, w_s, vec, left_vec, _, proj, tok_t):
    wide = w_k.shape[1] // 2
    n = proj.shape[0]
    total = None
    for w, kept, i in ((w_k, True, 0), (w_k, True, 1), (w_s, False, 0), (w_s, False, 1)):
        q = halves_of(vec, left_vec, chunk_at(kept, i, wide))
        w_hi, w_lo = split(w[:, i * wide : (i + 1) * wide])
        both = dot(q, w_hi, NT)
        term = both[:n] + both[n:] + dot(q[:n], w_lo, NT)
        total = term if total is None else total + term
    proj[...] = total
    tok_t[...] = tok_v[...].T


def norm_kernel(scale, i, own, got, cot, gain, vec, left_vec, on_keys_in, gain_in, _, kg, on_keys, gain_grad, passed):
    head = gain.shape[1]
    wide = own.shape[1]
    n = on_keys.shape[0]
    g = gain[...]
    start = chunk_at(True, i, wide).start
    total = gain_in[...]
    for h in range(wide // head):
        cols = slice(h * head, (h + 1) * head)
        keys = (own[:, cols].astype(F32) + got[:, cols].astype(F32)) * scale
        up = cot[:, pl.ds(pl.multiple_of(start + h * head, head), head)].astype(F32)
        gh = up * g
        inv = lax.rsqrt(jnp.mean(keys * keys, axis=-1, keepdims=True) + 1e-6)
        along = jnp.mean(gh * keys, axis=-1, keepdims=True)
        unit = keys * inv
        kg[:, cols] = (inv * (gh - unit * (inv * along))).astype(BF16)
        total = total + jnp.sum(up * unit, axis=0, keepdims=True)
    gain_grad[...] = total
    both = dot(halves_of(vec, left_vec, chunk_at(True, i, wide)), kg[...], NT)
    on_keys[...] = on_keys_in[...] + both[:n] + both[n:]


def odd_replica():
    return lax.rem(lax.axis_index("loop"), 2) == 0


def project_kernel(rate, mine, other, proj0, tok_v, first, second, out):
    hi, lo = split(mine[...] + other[...])
    rank = first.shape[0]
    n = 2 * rank
    both = dot(jnp.concatenate([hi, lo], axis=0), tok_v[...])
    proj = proj0[...] - rate * (both[:n] + both[n:])
    out[...] = proj
    odd = odd_replica()
    first[...] = jnp.where(odd, proj[:rank], proj[rank:])
    second[...] = jnp.where(odd, proj[rank:], proj[:rank])


def step_kernel(rate, i, tok_t, kg, w, out, out_hi, out_lo):
    wide = kg.shape[1]
    stepped = w[:, i * wide : (i + 1) * wide] - rate * dot(tok_t[...], kg[...])
    out[...] = stepped
    hi, lo = split(stepped)
    out_hi[...] = hi
    out_lo[...] = lo


def input_kernel(scale, kg_k0, kg_k1, kg_s0, kg_s1, hi_k, hi_s, _, out, stage, sem):
    wide = kg_k0.shape[1]
    steps = sem.shape[0]
    k = stage.shape[1] // steps
    copies = []
    for j in range(steps):
        at = slice(j * k, (j + 1) * k)
        total = None
        for kg, hi, i in ((kg_k0, hi_k, 0), (kg_k1, hi_k, 1), (kg_s0, hi_s, 0), (kg_s1, hi_s, 1)):
            term = dot(kg[...], hi[at, i * wide : (i + 1) * wide], NT)
            total = term if total is None else total + term
        stage[:, at] = (total * scale).astype(BF16)
        copies.append(pltpu.make_async_copy(stage.at[:, pl.ds(j * k, k)], out.at[:, pl.ds(j * k, k)], sem.at[j]))
        copies[j].start()
    for j in range(steps):
        copies[j].wait()


def back_kernel(proj, got_first, got_second, gain_grad, *refs):
    *blocks, rows_out, out = refs
    wide = blocks[0].shape[1]
    width = 4 * wide
    n = proj.shape[0]
    rank = n // 2
    odd = odd_replica()
    got_right = jnp.where(odd, got_first[...], got_second[...])
    got_left = jnp.where(odd, got_second[...], got_first[...])
    rows = jnp.concatenate([proj[:rank] - got_right, got_left - proj[rank:]], axis=0)
    rows_out[...] = rows
    r_hi, r_lo = split(rows)
    r = jnp.concatenate([r_hi, r_lo], axis=0)
    for j, (kept, i) in enumerate(((True, 0), (True, 1), (False, 0), (False, 1))):
        s_hi, s_lo = blocks[2 * j], blocks[2 * j + 1]
        both = dot(r, s_hi[...])
        out[:, chunk_at(kept, i, wide)] = both[:n] + both[n:] + dot(r_hi, s_lo[...])
    square = dot(r, r, NT)
    gram = (square[:n, :n] + square[n:, n:]) + (square[:n, n:] + square[n:, :n])
    out[:, width : width + 128] = jnp.concatenate([gram, jnp.zeros((n, 128 - n), F32)], axis=1)
    out[:, width + 128 :] = jnp.broadcast_to(gain_grad[...], (n, 128))


def pair_kernel(mine, other, keep, near, far, gain_grad):
    rank = keep.shape[0]
    width = mine.shape[1] - 256
    both = mine[...] + other[...]
    first = core_index() == 0
    keep[:, :width] = jnp.where(first, both[rank:, :width], both[:rank, :width])
    for e in range(2):
        keep[:, width + 128 * e : width + 128 * (e + 1)] = both[e * rank : (e + 1) * rank, width : width + 128]
    for aside in (near, far):
        aside[:, :width] = jnp.where(first, both[:rank, :width], both[rank:, :width])
        aside[:, width:] = jnp.zeros((rank, aside.shape[1] - width), F32)
    gain_grad[...] = both[0:1, width + 128 :]


def edge_kernel(keep, other, near, far, _, out, gram):
    rank, width = out.shape
    whole = keep[...] + other[...]
    beyond = near[:, :width] + far[:, :width]
    out[...] = jnp.where(core_index() == 0, beyond - whole[:, :width], whole[:, :width] - beyond)
    for e in range(2):
        gram[e * rank : (e + 1) * rank] = whole[:, width + 128 * e : width + 128 * (e + 1)]


def inverse_factor(gram, rank):
    n = gram.shape[0]
    width = gram.shape[1]
    lane = lax.broadcasted_iota(jnp.int32, (rank, width), 1)
    row = lax.broadcasted_iota(jnp.int32, (rank, width), 0)
    parts = []
    for e in range(n // rank):
        a = gram[e * rank : (e + 1) * rank]
        a = jnp.where((lane >= e * rank) & (lane < (e + 1) * rank), a, 0.0)
        a = jnp.where(lane == n + e * rank + row, 1.0, a)
        for i in range(rank):
            col = a[:, e * rank + i : e * rank + i + 1]
            pivot = lax.rsqrt(col[i : i + 1])
            line = a[i : i + 1] * pivot
            a = jnp.where(row == i, line, jnp.where(row > i, a - (col * pivot) * line, a))
        parts.append(a)
    return jnp.concatenate(parts, axis=0)


def apply_inverse(both, x, n):
    total = None
    for j in range(n):
        term = both[:, n + j : n + j + 1] * x[j : j + 1]
        total = term if total is None else total + term
    return total


def whiten_kernel(rank, gram, rows, gain, gain_grad, inverse, lhs, new_gain, stage, sem):
    stage[...] = gain[...] - 0.002 * gain_grad[...]
    copy = pltpu.make_async_copy(stage, new_gain, sem)
    copy.start()
    both = inverse_factor(gram[...], rank)
    inverse[...] = both
    u_hi, u_lo = split(apply_inverse(both, rows[...], 2 * rank))
    lhs[...] = jnp.concatenate([u_hi, u_hi, u_lo, jnp.zeros_like(u_hi)], axis=0).T
    copy.wait()


def mix_kernel(s_k0, s_k1, s_s0, s_s1, inverse, lhs, mine, other, out, new_vec, stage, vec_stage, right_side, sem, vec_sem):
    rank, width = vec_stage.shape
    depth, wide = s_k0.shape
    n = 2 * rank
    first = core_index() == 0
    a, b = mine[...], other[...]
    back = jnp.concatenate([jnp.where(first, b, a), jnp.where(first, a, b)], axis=0)
    nv = apply_inverse(inverse[...], back, n)
    sign = jnp.where(lax.broadcasted_iota(jnp.int32, (n, width), 0) < rank, 1.0 / 3.0, -1.0 / 3.0)
    v_hi, v_lo = split(nv * sign)
    right_side[...] = jnp.concatenate([v_hi, v_lo, v_hi, jnp.zeros_like(v_hi)], axis=0)
    vec_stage[...] = nv[:rank]
    vec_copy = pltpu.make_async_copy(vec_stage, new_vec, vec_sem)
    vec_copy.start()
    parts = sem.shape[0]
    k = depth // parts
    copies = []
    for p in range(parts):
        at = slice(p * k, (p + 1) * k)
        for s, kept, i in ((s_k0, True, 0), (s_k1, True, 1), (s_s0, False, 0), (s_s1, False, 1)):
            cols = chunk_at(kept, i, wide)
            stage[at, cols] = s[at] - dot(lhs[at], right_side[:, cols])
        copies.append(pltpu.make_async_copy(stage.at[pl.ds(p * k, k)], out.at[pl.ds(p * k, k)], sem.at[p]))
        copies[p].start()
    for copy in copies:
        copy.wait()
    vec_copy.wait()


def shards(tokens, weights, gain, cotangent, vectors):
    rows, depth = tokens.shape
    width = weights.shape[2]
    half = width // 2
    wide = half // 2
    rank = vectors.shape[1]
    n = 2 * rank
    tp = lax.axis_size("tp")
    loop = lax.axis_size("loop")
    scale = (depth * tp) ** -0.5
    rate = 0.1 * scale
    weight = weights[0]
    vec = vectors[0]
    core = [(i, i ^ 1) for i in range(tp)]
    chip = [(i, i ^ 2) for i in range(tp)]
    right = [(i, (i + 1) % loop) for i in range(loop)]
    odd_edges = [(i, (i + 1 if i % 2 else i - 1) % loop) for i in range(loop)]
    even_edges = [(i, i ^ 1) for i in range(loop)]
    along = [
        (i * tp + t, ((i + 1) % loop if t % 2 == 0 else (i - 1) % loop) * tp + t) for i in range(loop) for t in range(tp)
    ]
    along_far = [(i, j ^ 2) for i, j in along]
    dma = pltpu.SemaphoreType.DMA
    block, block16, keys16 = ((depth, wide), F32), ((depth, wide), BF16), ((rows, wide), BF16)
    steps = 5

    tok_v, w_s, hi_s, part = call(
        first_kernel,
        (tokens, weight),
        [((rows, depth), BF16), ((depth, half), F32), ((depth, half), BF16), ((rows, half), BF16)],
        [dma, dma((steps,))],
        spaces=(False, False),
    )
    from_core = lax.ppermute(part, "tp", core)
    w_k, hi_k, own = call(
        own_kernel,
        (tok_v, weight),
        [((depth, half), F32), ((depth, half), BF16), ((rows, half), F32)],
        [dma((steps,))],
        spaces=(True, False),
    )
    chip0, chip1 = call(chip_sum_kernel, (own, from_core), [keys16, keys16])
    from_chip0 = lax.ppermute(chip0, "tp", chip)
    from_chip1 = lax.ppermute(chip1, "tp", chip)
    left_vec = lax.ppermute(vec, "loop", right)
    proj0, tok_t = call(
        shadow_kernel,
        (tok_v, w_k, w_s, vec, left_vec, chip1),
        [((n, depth), F32), ((depth, rows), BF16)],
    )

    def norm(i, chip_part, from_chip, on_keys, gain_part, after):
        return call(
            functools.partial(norm_kernel, scale, i),
            (chip_part, from_chip, cotangent, gain, vec, left_vec, on_keys, gain_part, after),
            [keys16, ((n, rows), F32), (gain.shape, F32), (after.shape, after.dtype)],
            aliases={8: 3},
            nbytes=40 * MIB if i == 0 else 1,
        )

    def step(i, kg, w):
        return call(
            functools.partial(step_kernel, rate, i),
            (tok_t, kg, w),
            [block, block16, block16],
        )

    kg_k0, on_keys, gain_part, proj0 = norm(
        0, chip0, from_chip0, jnp.zeros((n, rows), F32), jnp.zeros(gain.shape, F32), proj0
    )
    s_k0, s_hi_k0, s_lo_k0 = step(0, kg_k0, w_k)
    kg_k1, on_keys, gain_part, s_lo_k0 = norm(1, chip1, from_chip1, on_keys, gain_part, s_lo_k0)
    on_keys_s = lax.ppermute(on_keys, "tp", core)
    s_k1, s_hi_k1, s_lo_k1 = step(1, kg_k1, w_k)
    kg_s0 = lax.ppermute(kg_k0, "tp", core)
    kg_s1 = lax.ppermute(kg_k1, "tp", core)
    first, second, proj = call(
        functools.partial(project_kernel, rate),
        (on_keys, on_keys_s, proj0, tok_v),
        [((rank, depth), F32), ((rank, depth), F32), ((n, depth), F32)],
        nbytes=40 * MIB,
    )
    got_first = lax.ppermute(first, "loop", even_edges)
    got_second = lax.ppermute(second, "loop", odd_edges)
    s_s0, s_hi_s0, s_lo_s0 = step(0, kg_s0, w_s)
    s_s1, s_hi_s1, s_lo_s1 = step(1, kg_s1, w_s)
    edge_rows, payload = call(
        back_kernel,
        (proj, got_first, got_second, gain_part)
        + (s_hi_k0, s_lo_k0, s_hi_k1, s_lo_k1, s_hi_s0, s_lo_s0, s_hi_s1, s_lo_s1),
        [((n, depth), F32), ((n, width + 256), F32)],
    )
    other_core = lax.ppermute(payload, "tp", core)
    keep, near, far, gain_grad = call(
        pair_kernel,
        (payload, other_core),
        [((rank, width + 256), F32), ((rank, width + 384), F32), ((rank, width + 512), F32), (gain.shape, F32)],
    )
    everyone = ("loop", "tp")
    far = lax.ppermute(far, everyone, along_far)
    near = lax.ppermute(near, everyone, along)
    other_chip = lax.ppermute(keep, "tp", chip)
    (input_grad,) = call(
        functools.partial(input_kernel, scale),
        (kg_k0, kg_k1, kg_s0, kg_s1, hi_k, hi_s, keep),
        [((rows, depth), BF16)],
        [pltpu.VMEM((rows, depth), BF16), dma((steps,))],
        out_spaces=(False,),
    )
    mine, gram = call(
        edge_kernel,
        (keep, other_chip, near, far, input_grad),
        [((rank, width), F32), ((n, 128), F32)],
        spaces=(True, True, True, True, False),
    )
    other = lax.ppermute(mine, "tp", core)
    inverse, lhs, new_gain = call(
        functools.partial(whiten_kernel, rank),
        (gram, edge_rows, gain, gain_grad),
        [((n, 128), F32), ((depth, 4 * n), BF16), (gain.shape, F32)],
        [pltpu.VMEM(gain.shape, F32), dma],
        out_spaces=(True, True, False),
    )
    parts = 10
    new_weights, new_vec = call(
        mix_kernel,
        (s_k0, s_k1, s_s0, s_s1, inverse, lhs, mine, other),
        [((depth, width), F32), ((rank, width), F32)],
        [
            pltpu.VMEM((depth, width), F32),
            pltpu.VMEM((rank, width), F32),
            pltpu.VMEM((4 * n, width), BF16),
            dma((parts,)),
            dma,
        ],
        out_spaces=(False, False),
    )
    return (new_weights[None], input_grad, new_gain, new_vec[None])


def solution(mesh):
    return jax.shard_map(
        shards,
        mesh=mesh,
        in_specs=(
            P("loop", "tp"),
            P("loop", "tp", None),
            P("loop", None),
            P("loop", None),
            P("loop", None, None),
        ),
        out_specs=(P("loop", "tp", None), P("loop", "tp"), P("loop", None), P("loop", None, None)),
        check_vma=False,
    )
```

```python
import functools

import jax
import jax.numpy as jnp
from jax import lax
from jax.experimental import pallas as pl
from jax.experimental.pallas import tpu as pltpu
from jax.sharding import PartitionSpec as P

F32 = jnp.float32
BF16 = jnp.bfloat16
MIB = 1024 * 1024
VM = pl.BlockSpec(memory_space=pltpu.VMEM)
ANY = pl.BlockSpec(memory_space=pl.ANY)
NT = (((1,), (1,)), ((), ()))


def in_vmem(x):
    return pltpu.with_memory_space_constraint(x, pltpu.VMEM)


def in_hbm(x):
    return pltpu.with_memory_space_constraint(x, pltpu.HBM)


def call(body, args, outs, scratch=(), limit=24, nbytes=1, spaces=None, out_spaces=None, aliases=None):
    spaces = spaces or (True,) * len(args)
    out_spaces = out_spaces or (True,) * len(outs)
    return pl.pallas_call(
        body,
        out_shape=[
            pltpu.VMEM(shape, dtype) if inside else pltpu.HBM(shape, dtype)
            for (shape, dtype), inside in zip(outs, out_spaces)
        ],
        in_specs=[VM if inside else ANY for inside in spaces],
        out_specs=[VM if inside else ANY for inside in out_spaces],
        scratch_shapes=list(scratch),
        input_output_aliases=aliases or {},
        compiler_params=pltpu.CompilerParams(vmem_limit_bytes=limit * MIB),
        cost_estimate=pl.CostEstimate(flops=400 * nbytes, bytes_accessed=nbytes, transcendentals=0),
    )(*[in_vmem(a) if inside else in_hbm(a) for a, inside in zip(args, spaces)])


def dot(a, b, dims=(((1,), (0,)), ((), ()))):
    return lax.dot_general(a, b, dims, preferred_element_type=F32)


def split(x):
    hi = x.astype(BF16)
    return hi, (x - hi.astype(F32)).astype(BF16)


def core_index():
    return lax.rem(lax.axis_index("tp"), 2)


def chunk_at(kept, i, wide):
    c = core_index()
    which = c if kept else 1 - c
    return pl.ds(pl.multiple_of(which * (2 * wide) + i * wide, 128), wide)


def half_in(w, to, kept, sems, beside=()):
    half = to.shape[1]
    steps = sems.shape[0]
    k = to.shape[0] // steps
    c = core_index()
    cols = pl.ds(pl.multiple_of((c if kept else 1 - c) * half, 128), half)
    copies = []
    for j in range(steps):
        at = pl.ds(j * k, k)
        copies.append(pltpu.make_async_copy(w.at[at, cols], to.at[at], sems.at[j]))
        for copy in beside[j : j + 1]:
            copy.start()
        copies[j].start()
    return copies


def partial(tok_v, w_v, hi_v, copies, beside=()):
    steps = len(copies)
    k = w_v.shape[0] // steps
    acc = None
    for j in range(steps):
        for copy in beside[j : j + 1]:
            copy.wait()
        copies[j].wait()
        at = slice(j * k, (j + 1) * k)
        hi = w_v[at].astype(BF16)
        hi_v[at] = hi
        term = dot(tok_v[:, at], hi)
        acc = term if acc is None else acc + term
    return acc


def first_kernel(tok, w, tok_v, w_s, hi_s, part, tok_sem, w_sem):
    steps = w_sem.shape[0]
    k = tok.shape[1] // steps
    tok_copies = []
    for j in range(steps):
        at = pl.ds(j * k, k)
        tok_copies.append(pltpu.make_async_copy(tok.at[:, at], tok_v.at[:, at], tok_sem.at[j]))
    copies = half_in(w, w_s, False, w_sem, tok_copies)
    part[...] = partial(tok_v, w_s, hi_s, copies, tok_copies).astype(BF16)


def own_kernel(tok_v, w, w_k, hi_k, own, w_sem):
    own[...] = partial(tok_v, w_k, hi_k, half_in(w, w_k, True, w_sem))


def chip_sum_kernel(own, got, out0, out1):
    wide = out0.shape[1]
    out0[...] = (own[:, :wide] + got[:, :wide].astype(F32)).astype(BF16)
    out1[...] = (own[:, wide:] + got[:, wide:].astype(F32)).astype(BF16)


def halves_of(vec, left_vec, at):
    hi, lo = split(jnp.concatenate([vec[:, at], left_vec[:, at]], axis=0))
    return jnp.concatenate([hi, lo], axis=0)


def shadow_kernel(tok_v, w_k, w_s, vec, left_vec, _, proj, tok_t):
    wide = w_k.shape[1] // 2
    n = proj.shape[0]
    total = None
    for w, kept, i in ((w_k, True, 0), (w_k, True, 1), (w_s, False, 0), (w_s, False, 1)):
        q = halves_of(vec, left_vec, chunk_at(kept, i, wide))
        w_hi, w_lo = split(w[:, i * wide : (i + 1) * wide])
        both = dot(q, w_hi, NT)
        term = both[:n] + both[n:] + dot(q[:n], w_lo, NT)
        total = term if total is None else total + term
    proj[...] = total
    tok_t[...] = tok_v[...].T


def norm_kernel(scale, i, own, got, cot, gain, vec, left_vec, on_keys_in, gain_in, _, kg, on_keys, gain_grad, passed):
    head = gain.shape[1]
    wide = own.shape[1]
    n = on_keys.shape[0]
    g = gain[...]
    start = chunk_at(True, i, wide).start
    total = gain_in[...]
    for h in range(wide // head):
        cols = slice(h * head, (h + 1) * head)
        keys = (own[:, cols].astype(F32) + got[:, cols].astype(F32)) * scale
        up = cot[:, pl.ds(pl.multiple_of(start + h * head, head), head)].astype(F32)
        gh = up * g
        inv = lax.rsqrt(jnp.mean(keys * keys, axis=-1, keepdims=True) + 1e-6)
        along = jnp.mean(gh * keys, axis=-1, keepdims=True)
        unit = keys * inv
        kg[:, cols] = (inv * (gh - unit * (inv * along))).astype(BF16)
        total = total + jnp.sum(up * unit, axis=0, keepdims=True)
    gain_grad[...] = total
    both = dot(halves_of(vec, left_vec, chunk_at(True, i, wide)), kg[...], NT)
    on_keys[...] = on_keys_in[...] + both[:n] + both[n:]


def odd_replica():
    return lax.rem(lax.axis_index("loop"), 2) == 0


def project_kernel(rate, mine, other, proj0, tok_v, first, second, out):
    hi, lo = split(mine[...] + other[...])
    rank = first.shape[0]
    n = 2 * rank
    both = dot(jnp.concatenate([hi, lo], axis=0), tok_v[...])
    proj = proj0[...] - rate * (both[:n] + both[n:])
    out[...] = proj
    odd = odd_replica()
    first[...] = jnp.where(odd, proj[:rank], proj[rank:])
    second[...] = jnp.where(odd, proj[rank:], proj[:rank])


def step_kernel(rate, i, tok_t, kg, w, out, out_hi, out_lo):
    wide = kg.shape[1]
    stepped = w[:, i * wide : (i + 1) * wide] - rate * dot(tok_t[...], kg[...])
    out[...] = stepped
    hi, lo = split(stepped)
    out_hi[...] = hi
    out_lo[...] = lo


def input_kernel(scale, kg_k0, kg_k1, kg_s0, kg_s1, hi_k, hi_s, _, out, stage, sem):
    wide = kg_k0.shape[1]
    steps = sem.shape[0]
    k = stage.shape[1] // steps
    copies = []
    for j in range(steps):
        at = slice(j * k, (j + 1) * k)
        total = None
        for kg, hi, i in ((kg_k0, hi_k, 0), (kg_k1, hi_k, 1), (kg_s0, hi_s, 0), (kg_s1, hi_s, 1)):
            term = dot(kg[...], hi[at, i * wide : (i + 1) * wide], NT)
            total = term if total is None else total + term
        stage[:, at] = (total * scale).astype(BF16)
        copies.append(pltpu.make_async_copy(stage.at[:, pl.ds(j * k, k)], out.at[:, pl.ds(j * k, k)], sem.at[j]))
        copies[j].start()
    for j in range(steps):
        copies[j].wait()


def back_kernel(proj, got_first, got_second, gain_grad, *refs):
    *blocks, rows_out, out = refs
    wide = blocks[0].shape[1]
    width = 4 * wide
    n = proj.shape[0]
    rank = n // 2
    odd = odd_replica()
    got_right = jnp.where(odd, got_first[...], got_second[...])
    got_left = jnp.where(odd, got_second[...], got_first[...])
    rows = jnp.concatenate([proj[:rank] - got_right, got_left - proj[rank:]], axis=0)
    rows_out[...] = rows
    r_hi, r_lo = split(rows)
    r = jnp.concatenate([r_hi, r_lo], axis=0)
    for j, (kept, i) in enumerate(((True, 0), (True, 1), (False, 0), (False, 1))):
        s_hi, s_lo = blocks[2 * j], blocks[2 * j + 1]
        both = dot(r, s_hi[...])
        out[:, chunk_at(kept, i, wide)] = both[:n] + both[n:] + dot(r_hi, s_lo[...])
    square = dot(r, r, NT)
    gram = (square[:n, :n] + square[n:, n:]) + (square[:n, n:] + square[n:, :n])
    out[:, width : width + 128] = jnp.concatenate([gram, jnp.zeros((n, 128 - n), F32)], axis=1)
    out[:, width + 128 :] = jnp.broadcast_to(gain_grad[...], (n, 128))


def pair_kernel(mine, other, keep, near, far, gain_grad):
    rank = keep.shape[0]
    width = mine.shape[1] - 256
    both = mine[...] + other[...]
    first = core_index() == 0
    keep[:, :width] = jnp.where(first, both[rank:, :width], both[:rank, :width])
    for e in range(2):
        keep[:, width + 128 * e : width + 128 * (e + 1)] = both[e * rank : (e + 1) * rank, width : width + 128]
    for aside in (near, far):
        aside[:, :width] = jnp.where(first, both[:rank, :width], both[rank:, :width])
        aside[:, width:] = jnp.zeros((rank, aside.shape[1] - width), F32)
    gain_grad[...] = both[0:1, width + 128 :]


def edge_kernel(keep, other, near, far, _, out, gram):
    rank, width = out.shape
    whole = keep[...] + other[...]
    beyond = near[:, :width] + far[:, :width]
    out[...] = jnp.where(core_index() == 0, beyond - whole[:, :width], whole[:, :width] - beyond)
    for e in range(2):
        gram[e * rank : (e + 1) * rank] = whole[:, width + 128 * e : width + 128 * (e + 1)]


def inverse_factor(gram, rank):
    n = gram.shape[0]
    width = gram.shape[1]
    lane = lax.broadcasted_iota(jnp.int32, (rank, width), 1)
    row = lax.broadcasted_iota(jnp.int32, (rank, width), 0)
    parts = []
    for e in range(n // rank):
        a = gram[e * rank : (e + 1) * rank]
        a = jnp.where((lane >= e * rank) & (lane < (e + 1) * rank), a, 0.0)
        a = jnp.where(lane == n + e * rank + row, 1.0, a)
        for i in range(rank):
            col = a[:, e * rank + i : e * rank + i + 1]
            pivot = lax.rsqrt(col[i : i + 1])
            line = a[i : i + 1] * pivot
            a = jnp.where(row == i, line, jnp.where(row > i, a - (col * pivot) * line, a))
        parts.append(a)
    return jnp.concatenate(parts, axis=0)


def apply_inverse(both, x, n):
    total = None
    for j in range(n):
        term = both[:, n + j : n + j + 1] * x[j : j + 1]
        total = term if total is None else total + term
    return total


def whiten_kernel(rank, gram, rows, gain, gain_grad, inverse, lhs, new_gain, stage, sem):
    stage[...] = gain[...] - 0.002 * gain_grad[...]
    copy = pltpu.make_async_copy(stage, new_gain, sem)
    copy.start()
    both = inverse_factor(gram[...], rank)
    inverse[...] = both
    u_hi, u_lo = split(apply_inverse(both, rows[...], 2 * rank))
    lhs[...] = jnp.concatenate([u_hi, u_hi, u_lo, jnp.zeros_like(u_hi)], axis=0).T
    copy.wait()


def last_blocks(depth):
    short = depth // 20
    return [0, short] + list(range(2 * short, depth, 4 * short)) + [depth]


def mix_kernel(s_k0, s_k1, s_s0, s_s1, inverse, lhs, mine, other, out, new_vec, stage, vec_stage, right_side, sem, vec_sem):
    rank, width = vec_stage.shape
    depth, wide = s_k0.shape
    n = 2 * rank
    first = core_index() == 0
    a, b = mine[...], other[...]
    back = jnp.concatenate([jnp.where(first, b, a), jnp.where(first, a, b)], axis=0)
    nv = apply_inverse(inverse[...], back, n)
    sign = jnp.where(lax.broadcasted_iota(jnp.int32, (n, width), 0) < rank, 1.0 / 3.0, -1.0 / 3.0)
    v_hi, v_lo = split(nv * sign)
    right_side[...] = jnp.concatenate([v_hi, v_lo, v_hi, jnp.zeros_like(v_hi)], axis=0)
    vec_stage[...] = nv[:rank]
    vec_copy = pltpu.make_async_copy(vec_stage, new_vec, vec_sem)
    vec_copy.start()
    copies = []
    ends = last_blocks(depth)
    for p, (lo, hi) in enumerate(zip(ends[:-1], ends[1:])):
        at = slice(lo, hi)
        for s, kept, i in ((s_k0, True, 0), (s_k1, True, 1), (s_s0, False, 0), (s_s1, False, 1)):
            cols = chunk_at(kept, i, wide)
            stage[at, cols] = s[at] - dot(lhs[at], right_side[:, cols])
        rows_out = pl.ds(lo, hi - lo)
        copies.append(pltpu.make_async_copy(stage.at[rows_out], out.at[rows_out], sem.at[p]))
        copies[p].start()
    for copy in copies:
        copy.wait()
    vec_copy.wait()


def shards(tokens, weights, gain, cotangent, vectors):
    rows, depth = tokens.shape
    width = weights.shape[2]
    half = width // 2
    wide = half // 2
    rank = vectors.shape[1]
    n = 2 * rank
    tp = lax.axis_size("tp")
    loop = lax.axis_size("loop")
    scale = (depth * tp) ** -0.5
    rate = 0.1 * scale
    weight = weights[0]
    vec = vectors[0]
    core = [(i, i ^ 1) for i in range(tp)]
    chip = [(i, i ^ 2) for i in range(tp)]
    right = [(i, (i + 1) % loop) for i in range(loop)]
    odd_edges = [(i, (i + 1 if i % 2 else i - 1) % loop) for i in range(loop)]
    even_edges = [(i, i ^ 1) for i in range(loop)]
    along = [
        (i * tp + t, ((i + 1) % loop if t % 2 == 0 else (i - 1) % loop) * tp + t) for i in range(loop) for t in range(tp)
    ]
    along_far = [(i, j ^ 2) for i, j in along]
    dma = pltpu.SemaphoreType.DMA
    block, block16, keys16 = ((depth, wide), F32), ((depth, wide), BF16), ((rows, wide), BF16)
    steps = 5

    tok_v, w_s, hi_s, part = call(
        first_kernel,
        (tokens, weight),
        [((rows, depth), BF16), ((depth, half), F32), ((depth, half), BF16), ((rows, half), BF16)],
        [dma((steps,)), dma((steps,))],
        spaces=(False, False),
    )
    from_core = lax.ppermute(part, "tp", core)
    w_k, hi_k, own = call(
        own_kernel,
        (tok_v, weight),
        [((depth, half), F32), ((depth, half), BF16), ((rows, half), F32)],
        [dma((steps,))],
        spaces=(True, False),
    )
    chip0, chip1 = call(chip_sum_kernel, (own, from_core), [keys16, keys16])
    from_chip0 = lax.ppermute(chip0, "tp", chip)
    from_chip1 = lax.ppermute(chip1, "tp", chip)
    left_vec = lax.ppermute(vec, "loop", right)
    proj0, tok_t = call(
        shadow_kernel,
        (tok_v, w_k, w_s, vec, left_vec, chip1),
        [((n, depth), F32), ((depth, rows), BF16)],
    )

    def norm(i, chip_part, from_chip, on_keys, gain_part, after):
        return call(
            functools.partial(norm_kernel, scale, i),
            (chip_part, from_chip, cotangent, gain, vec, left_vec, on_keys, gain_part, after),
            [keys16, ((n, rows), F32), (gain.shape, F32), (after.shape, after.dtype)],
            aliases={8: 3},
            nbytes=40 * MIB if i == 0 else 1,
        )

    def step(i, kg, w):
        return call(
            functools.partial(step_kernel, rate, i),
            (tok_t, kg, w),
            [block, block16, block16],
        )

    kg_k0, on_keys, gain_part, proj0 = norm(
        0, chip0, from_chip0, jnp.zeros((n, rows), F32), jnp.zeros(gain.shape, F32), proj0
    )
    s_k0, s_hi_k0, s_lo_k0 = step(0, kg_k0, w_k)
    kg_k1, on_keys, gain_part, s_lo_k0 = norm(1, chip1, from_chip1, on_keys, gain_part, s_lo_k0)
    on_keys_s = lax.ppermute(on_keys, "tp", core)
    s_k1, s_hi_k1, s_lo_k1 = step(1, kg_k1, w_k)
    kg_s0 = lax.ppermute(kg_k0, "tp", core)
    kg_s1 = lax.ppermute(kg_k1, "tp", core)
    first, second, proj = call(
        functools.partial(project_kernel, rate),
        (on_keys, on_keys_s, proj0, tok_v),
        [((rank, depth), F32), ((rank, depth), F32), ((n, depth), F32)],
        nbytes=40 * MIB,
    )
    got_first = lax.ppermute(first, "loop", even_edges)
    got_second = lax.ppermute(second, "loop", odd_edges)
    s_s0, s_hi_s0, s_lo_s0 = step(0, kg_s0, w_s)
    s_s1, s_hi_s1, s_lo_s1 = step(1, kg_s1, w_s)
    edge_rows, payload = call(
        back_kernel,
        (proj, got_first, got_second, gain_part)
        + (s_hi_k0, s_lo_k0, s_hi_k1, s_lo_k1, s_hi_s0, s_lo_s0, s_hi_s1, s_lo_s1),
        [((n, depth), F32), ((n, width + 256), F32)],
    )
    other_core = lax.ppermute(payload, "tp", core)
    keep, near, far, gain_grad = call(
        pair_kernel,
        (payload, other_core),
        [((rank, width + 256), F32), ((rank, width + 384), F32), ((rank, width + 512), F32), (gain.shape, F32)],
    )
    everyone = ("loop", "tp")
    far = lax.ppermute(far, everyone, along_far)
    near = lax.ppermute(near, everyone, along)
    other_chip = lax.ppermute(keep, "tp", chip)
    (input_grad,) = call(
        functools.partial(input_kernel, scale),
        (kg_k0, kg_k1, kg_s0, kg_s1, hi_k, hi_s, keep),
        [((rows, depth), BF16)],
        [pltpu.VMEM((rows, depth), BF16), dma((steps,))],
        out_spaces=(False,),
    )
    mine, gram = call(
        edge_kernel,
        (keep, other_chip, near, far, input_grad),
        [((rank, width), F32), ((n, 128), F32)],
        spaces=(True, True, True, True, False),
    )
    other = lax.ppermute(mine, "tp", core)
    inverse, lhs, new_gain = call(
        functools.partial(whiten_kernel, rank),
        (gram, edge_rows, gain, gain_grad),
        [((n, 128), F32), ((depth, 4 * n), BF16), (gain.shape, F32)],
        [pltpu.VMEM(gain.shape, F32), dma],
        out_spaces=(True, True, False),
    )
    parts = len(last_blocks(depth)) - 1
    new_weights, new_vec = call(
        mix_kernel,
        (s_k0, s_k1, s_s0, s_s1, inverse, lhs, mine, other),
        [((depth, width), F32), ((rank, width), F32)],
        [
            pltpu.VMEM((depth, width), F32),
            pltpu.VMEM((rank, width), F32),
            pltpu.VMEM((4 * n, width), BF16),
            dma((parts,)),
            dma,
        ],
        out_spaces=(False, False),
    )
    return (new_weights[None], input_grad, new_gain, new_vec[None])


def solution(mesh):
    return jax.shard_map(
        shards,
        mesh=mesh,
        in_specs=(
            P("loop", "tp"),
            P("loop", "tp", None),
            P("loop", None),
            P("loop", None),
            P("loop", None, None),
        ),
        out_specs=(P("loop", "tp", None), P("loop", "tp"), P("loop", None), P("loop", None, None)),
        check_vma=False,
    )
```
